512 devices in a mesh: ctx: 64 (over y, z_lo, core), hid: 8 (over x, z_hi).
Axes of the slice: x: 4, y: 8, z: 8 (z_hi: 2, z_lo: 4; z = z_hi * 4 + z_lo), core: 2. Of those that a mesh axis runs over, the one named last changes fastest.
Arguments:
- q_act: bfloat16 [8192, 8192], P('ctx', 'hid'), may hold values from -6 to 6
- k_act: bfloat16 [8192, 8192], P('ctx', 'hid'), may hold values from -6 to 6
- v_act: bfloat16 [8192, 8192], P('ctx', 'hid'), may hold values from -6 to 6
- filt: float32 [128, 8192], P(None, 'hid'), may hold values from -0.5 to 0.5
- gain: float32 [8192], P('hid'), may hold values from 0.1 to 1.9
- segments: int32 [8192], P('ctx'), may hold values from 0 to 31, as said below
- grad_out: bfloat16 [8192, 8192], P('ctx', 'hid'), may hold values from -6 to 6
Outputs:
- layer_out: bfloat16 [8192, 8192], P('ctx', 'hid')
- q_grad: bfloat16 [8192, 8192], P('ctx', 'hid')
- k_grad: bfloat16 [8192, 8192], P('ctx', 'hid')
- v_grad: bfloat16 [8192, 8192], P('ctx', 'hid')
- filt_grad: float32 [128, 8192], P(None, 'hid')
- gain_grad: float32 [8192], P('hid')
The draws below stay inside these ranges and needn't reach their ends.
Inputs may be any that keep to these rules, and one draw needn't show every extreme that they name: `segments`: ids start at 0, never fall and rise by at most one from one position to the next; there are exactly 32 documents, each spanning at least 128 positions.
All inputs are finite; a program needn't handle non-finite values.
Results may differ from the reference program's by a relative error of at most 0.005.
Values may be sent and summed in bfloat16 or wider, within the bound.
No kernel may reach another device: no remote copies, remote signals or barrier semaphores. Data moves between devices by JAX's collectives and lax.ppermute only.
A program may use at most 64 MiB of HBM per device.

```python
import jax
import jax.numpy as jnp
from jax import lax

C = 8192
TAPS = 128
TOKENS = 8192


def draw_segments(key, part):
    key = jax.random.fold_in(key, 11)
    doc_count = TOKENS // (2 * TAPS)
    spare_rows = TOKENS - doc_count * TAPS
    cut_points = jnp.sort(jax.random.randint(key, (doc_count - 1,), 0, spare_rows + 1))
    doc_starts = jnp.arange(1, doc_count, dtype=jnp.int32) * TAPS + cut_points
    positions = jnp.arange(TOKENS, dtype=jnp.int32)
    doc_ids = jnp.sum((positions[:, None] >= doc_starts[None, :]).astype(jnp.int32), axis=1)
    return doc_ids.astype(jnp.int32)


def block_levels(own_key, shape, cuts, low, top_value):
    factor_of = 1.0
    for axis_at, parts in cuts:
        draws = jax.random.uniform(jax.random.fold_in(jax.random.fold_in(own_key, 6), axis_at), (parts,), jnp.float32, low / len(cuts), top_value / len(cuts))
        factor_of = factor_of * jnp.repeat(jnp.exp(draws), shape[axis_at] // parts).reshape((-1,) + (1,) * (len(shape) - 1 - axis_at))
    return factor_of


def gaussian(stream_key, extent, width, limit, shards=(), held_as=jnp.bfloat16):
    result = width * jax.random.normal(stream_key, extent, jnp.float32)
    if shards:
        result = result * block_levels(stream_key, extent, shards, -0.22, 0.18)
    return jnp.clip(result, -limit, limit).astype(held_as)


def setup_inputs(seed: int = 0) -> dict:
    key_of = jax.random.split(jax.random.key(seed), 8)
    q_act = gaussian(key_of[0], (TOKENS, C), 1.0, 6.0, ((0, 64), (1, 8)))
    k_act = gaussian(key_of[1], (TOKENS, C), 1.0, 6.0, ((0, 64), (1, 8)))
    v_act = gaussian(key_of[2], (TOKENS, C), 1.0, 6.0, ((0, 64), (1, 8)))
    filt = gaussian(key_of[3], (TAPS, C), TAPS ** -0.5, 0.5, ((1, 8),), jnp.float32)
    gain = jnp.clip(1.0 + 0.18 * jax.random.normal(key_of[4], (C,), jnp.float32), 0.1, 1.9)
    segments = draw_segments(jax.random.fold_in(key_of[7], 71), 0)
    grad_out = gaussian(key_of[6], (TOKENS, C), 1.0, 6.0, ((0, 64), (1, 8)))
    return {"q_act": q_act, "k_act": k_act, "v_act": v_act, "filt": filt, "gain": gain, "segments": segments, "grad_out": grad_out}


def reference(q_act, k_act, v_act, filt, gain, segments, grad_out):
    reach = TAPS - 1
    seg_ids = segments.astype(jnp.int32)
    prod = (k_act.astype(jnp.float32) * v_act.astype(jnp.float32)).astype(jnp.bfloat16)
    prod_pad = jnp.concatenate([jnp.zeros((reach, C), jnp.bfloat16), prod]).astype(jnp.float32)
    seg_before = jnp.concatenate([jnp.full((reach,), -1, jnp.int32), seg_ids])
    seg_after = jnp.concatenate([seg_ids, jnp.full((reach,), -1, jnp.int32)])

    def forward_tap(step, total):
        offset = (reach - step).astype(jnp.int32)
        source = lax.dynamic_slice_in_dim(prod_pad, offset, TOKENS, 0)
        match = (lax.dynamic_slice_in_dim(seg_before, offset, TOKENS, 0) == seg_ids).astype(jnp.float32)
        return total + filt[step][None, :] * source * match[:, None]
    conv = lax.fori_loop(0, TAPS, forward_tap, jnp.zeros((TOKENS, C), jnp.float32))
    query = q_act.astype(jnp.float32)
    y = query * conv
    rinv = lax.rsqrt(lax.optimization_barrier(jnp.sum(y * y, axis=1)) / C + 1e-06)
    layer_out = (y * rinv[:, None] * gain).astype(jnp.bfloat16)
    upstream = grad_out.astype(jnp.float32)
    scaled_up = upstream * gain
    gain_grad = lax.optimization_barrier(jnp.sum(upstream * y * rinv[:, None], axis=0))
    inner = lax.optimization_barrier(jnp.sum(scaled_up * y, axis=1))
    dy = rinv[:, None] * scaled_up - y * (rinv ** 3 * inner / C)[:, None]
    q_grad = (dy * conv).astype(jnp.bfloat16)
    dconv = (dy * query).astype(jnp.bfloat16)
    dconv_wide = dconv.astype(jnp.float32)
    dconv_pad = jnp.concatenate([dconv, jnp.zeros((reach, C), jnp.bfloat16)]).astype(jnp.float32)

    def backward_tap(step, carry):
        total, taps_grad = carry
        index = step.astype(jnp.int32)
        source = lax.dynamic_slice_in_dim(dconv_pad, index, TOKENS, 0)
        match = (lax.dynamic_slice_in_dim(seg_after, index, TOKENS, 0) == seg_ids).astype(jnp.float32)
        total = total + filt[step][None, :] * source * match[:, None]
        offset = (reach - step).astype(jnp.int32)
        earlier = lax.dynamic_slice_in_dim(prod_pad, offset, TOKENS, 0)
        back_match = (lax.dynamic_slice_in_dim(seg_before, offset, TOKENS, 0) == seg_ids).astype(jnp.float32)
        row = lax.optimization_barrier(jnp.sum(dconv_wide * earlier * back_match[:, None], axis=0))
        taps_grad = lax.dynamic_update_slice_in_dim(taps_grad, row[None, :], index, 0)
        return (total, taps_grad)
    dprod, filt_grad = lax.fori_loop(0, TAPS, backward_tap, (jnp.zeros((TOKENS, C), jnp.float32), jnp.zeros((TAPS, C), jnp.float32)))
    k_grad = (dprod * v_act.astype(jnp.float32)).astype(jnp.bfloat16)
    v_grad = (dprod * k_act.astype(jnp.float32)).astype(jnp.bfloat16)
    return (layer_out, q_grad, k_grad, v_grad, filt_grad, gain_grad)
```

```python
import jax
import jax.numpy as jnp
import ml_dtypes
import numpy as np
from jax import lax
from jax.experimental import pallas as pl
from jax.experimental.pallas import tpu as pltpu
from jax.sharding import PartitionSpec as P

C = 8192
ROWS = 128
FREQ = 128
BLOCK = 256


def split_const(matrix):
    high = matrix.astype(ml_dtypes.bfloat16)
    low = (matrix - high.astype(np.float64)).astype(ml_dtypes.bfloat16)
    return high, low


def transforms():
    omega = 2.0 * np.pi * (np.arange(FREQ) + 0.5) / (2 * FREQ)

    def at(positions):
        angle = omega[:, None] * positions[None, :]
        return np.concatenate([np.cos(angle), -np.sin(angle)], axis=0)

    here = np.arange(ROWS)
    own = at(here)
    left = at(here - ROWS)
    left[:, 0] = 0.0
    right = at(here + ROWS)
    right[:, -1] = 0.0
    own_hl = np.concatenate(split_const(own), axis=1)
    left_hl = np.concatenate(split_const(left), axis=1)
    right_hl = np.concatenate(split_const(right), axis=1)
    back_hl = np.concatenate(split_const(own.T / FREQ), axis=0)
    return own_hl, left_hl, right_hl, back_hl


def mm(a, b):
    return jnp.dot(a, b, preferred_element_type=jnp.float32)


def forward(matrix_hl, x):
    return mm(matrix_hl, jnp.concatenate([x, x], axis=0))


def forward_wide(matrix_hl, x):
    high = x.astype(jnp.bfloat16)
    low = (x - high.astype(jnp.float32)).astype(jnp.bfloat16)
    return forward(matrix_hl, high) + mm(matrix_hl[:, :ROWS], low)


def backward(back_hl, spectrum):
    high = spectrum.astype(jnp.bfloat16)
    low = (spectrum - high.astype(jnp.float32)).astype(jnp.bfloat16)
    both = mm(back_hl, high)
    return both[:ROWS] + both[ROWS:] + mm(back_hl[:ROWS], low)


def times(a, b):
    ar, ai, br, bi = a[:FREQ], a[FREQ:], b[:FREQ], b[FREQ:]
    return jnp.concatenate([ar * br - ai * bi, ar * bi + ai * br], axis=0)


def times_conj(a, b):
    ar, ai, br, bi = a[:FREQ], a[FREQ:], b[:FREQ], b[FREQ:]
    return jnp.concatenate([ar * br + ai * bi, ai * br - ar * bi], axis=0)


def down(row, width):
    square = jnp.broadcast_to(row, (ROWS, ROWS)).T
    return jnp.concatenate([square] * (width // ROWS), axis=1)


def first_doc(seg):
    return (seg == seg[:, :1]).astype(jnp.float32)


def last_doc(seg):
    return (seg == seg[:, ROWS - 1 :]).astype(jnp.float32)


def product(k_ref, v_ref):
    return (k_ref[...].astype(jnp.float32) * v_ref[...].astype(jnp.float32)).astype(jnp.bfloat16)


def conv_kernel(own_ref, left_ref, back_ref, seg_ref, k_ref, v_ref, halo_ref, filt_ref, q_ref, g_ref, gain_ref, conv_ref, stats_ref, sums):
    step = pl.program_id(0)
    width = k_ref.shape[1]
    seg = seg_ref[...]
    own, left, back = own_ref[...], left_ref[...], back_ref[...]
    in_first = down(first_doc(seg), width)
    prod = product(k_ref, v_ref)
    rest = prod * (1.0 - in_first).astype(jnp.bfloat16)
    parity = (seg[:, :1] % 2).astype(jnp.float32)
    joined = (halo_ref[0:1, :].astype(jnp.float32) == parity).astype(jnp.float32)
    taps = forward_wide(own, filt_ref[...])
    all_spec = forward(own, prod) + forward(left, halo_ref[...]) * joined
    rest_spec = forward(own, rest)
    conv_first = backward(back, times(all_spec, taps))
    conv_rest = backward(back, times(rest_spec, taps))
    conv = jnp.where(in_first > 0.5, conv_first, conv_rest)
    conv_ref[...] = conv
    y = q_ref[...].astype(jnp.float32) * conv
    gy = g_ref[...].astype(jnp.float32) * gain_ref[...]
    square, inner = y * y, gy * y
    square = sum(square[:, i * ROWS : (i + 1) * ROWS] for i in range(width // ROWS))
    inner = sum(inner[:, i * ROWS : (i + 1) * ROWS] for i in range(width // ROWS))

    @pl.when(step == 0)
    def _():
        sums[0] = square
        sums[1] = inner

    @pl.when(step > 0)
    def _():
        sums[0] += square
        sums[1] += inner

    @pl.when(step == pl.num_programs(0) - 1)
    def _():
        rows = jnp.concatenate(
            [jnp.sum(sums[0].T, axis=0, keepdims=True), jnp.sum(sums[1].T, axis=0, keepdims=True)], axis=0
        )
        stats_ref[...] = jnp.broadcast_to(rows[None], stats_ref.shape)


def scales(stats_ref):
    total = jnp.sum(stats_ref[...], axis=0)
    rinv = lax.rsqrt(total[0:1] / C + 1e-06)
    return rinv, rinv * rinv * rinv * total[1:2] / C


def grad_kernel(own_ref, left_ref, back_ref, seg_ref, k_ref, v_ref, halo_ref, q_ref, g_ref, gain_ref, conv_ref, stats_ref, chunk_ref, dconv_ref, head_ref):
    width = k_ref.shape[1]
    seg = seg_ref[...]
    own, left, back = own_ref[...], left_ref[...], back_ref[...]
    rinv, slope = scales(stats_ref)
    rinv, slope = down(rinv, width), down(slope, width)
    in_first = down(first_doc(seg), width)
    query = q_ref[...].astype(jnp.float32)
    up = g_ref[...].astype(jnp.float32)
    y = query * conv_ref[...]
    dy = rinv * (up * gain_ref[...]) - y * slope
    dconv = (dy * query).astype(jnp.bfloat16)
    dconv_ref[...] = dconv
    first_half = in_first.astype(jnp.bfloat16)
    d_first = dconv * first_half
    row = lax.broadcasted_iota(jnp.int32, (ROWS, width), 0)
    parity = (seg[:, :1] % 2).astype(jnp.float32)
    head_ref[...] = jnp.where(row == ROWS - 1, parity, d_first.astype(jnp.float32)).astype(jnp.bfloat16)
    d_rest = dconv - d_first
    prod = product(k_ref, v_ref)
    rest = prod * (1.0 - in_first).astype(jnp.bfloat16)
    joined = (halo_ref[0:1, :].astype(jnp.float32) == parity).astype(jnp.float32)
    all_spec = forward(own, prod) + forward(left, halo_ref[...]) * joined
    rest_spec = forward(own, rest)
    spectrum = times_conj(forward(own, d_first), all_spec) + times_conj(forward(own, d_rest), rest_spec)
    taps = backward(back, spectrum).astype(jnp.bfloat16)
    gain_sum = jnp.sum(up * y * rinv, axis=0, keepdims=True)
    gain_high = gain_sum.astype(jnp.bfloat16)
    gain_low = (gain_sum - gain_high.astype(jnp.float32)).astype(jnp.bfloat16)
    gain_both = jnp.concatenate([gain_high, gain_low], axis=0)
    for block in range(width // ROWS):
        lanes = slice(block * ROWS, (block + 1) * ROWS)
        for group in range(8):
            for pair in range(8):
                at = group * 16 + pair * 2
                chunk_ref[group, block, pair] = taps[at : at + 2, lanes]
            chunk_ref[group, block, 8] = gain_both[:, lanes]


def out_kernel(own_ref, right_ref, back_ref, seg_ref, k_ref, v_ref, q_ref, g_ref, gain_ref, conv_ref, stats_ref, dconv_ref, tail_ref, filt_ref, layer_ref, qg_ref, kg_ref, vg_ref):
    width = k_ref.shape[1]
    seg = seg_ref[...]
    own, right, back = own_ref[...], right_ref[...], back_ref[...]
    rinv, slope = scales(stats_ref)
    rinv, slope = down(rinv, width), down(slope, width)
    conv = conv_ref[...]
    y = q_ref[...].astype(jnp.float32) * conv
    gain = gain_ref[...]
    dy = rinv * (g_ref[...].astype(jnp.float32) * gain) - y * slope
    layer_ref[...] = (y * rinv * gain).astype(jnp.bfloat16)
    qg_ref[...] = (dy * conv).astype(jnp.bfloat16)
    dconv = dconv_ref[...]
    in_first = down(first_doc(seg), width)
    in_last = down(last_doc(seg), width)
    parity = (seg[:, ROWS - 1 :] % 2).astype(jnp.float32)
    joined = (tail_ref[ROWS - 1 :, :].astype(jnp.float32) == parity).astype(jnp.float32)
    taps = forward_wide(own, filt_ref[...])
    first_spec = forward(own, dconv * in_first.astype(jnp.bfloat16))
    all_spec = forward(own, dconv) + forward(right, tail_ref[...]) * joined
    dprod_last = backward(back, times_conj(all_spec, taps))
    dprod_first = backward(back, times_conj(first_spec, taps))
    dprod = jnp.where(in_last > 0.5, dprod_last, dprod_first)
    kg_ref[...] = (dprod * v_ref[...].astype(jnp.float32)).astype(jnp.bfloat16)
    vg_ref[...] = (dprod * k_ref[...].astype(jnp.float32)).astype(jnp.bfloat16)


def whole(shape):
    return pl.BlockSpec(shape, lambda i: (0,) * len(shape))


def columns(rows):
    return pl.BlockSpec((rows, BLOCK), lambda i: (0, i))


def params():
    return pltpu.CompilerParams(vmem_limit_bytes=48 * 1024 * 1024, dimension_semantics=("arbitrary",))


def cost(flops, moved):
    return pl.CostEstimate(flops=flops, bytes_accessed=moved, transcendentals=0)


def shifted(value, axis, steps):
    count = lax.axis_size(axis)
    first, last = (max(0, -steps), min(count, count - steps))
    return lax.ppermute(value, axis, [(source, source + steps) for source in range(first, last)])


def local(q_act, k_act, v_act, filt, gain, segments, grad_out):
    width = q_act.shape[1]
    n_ctx, n_hid = lax.axis_size("ctx"), lax.axis_size("hid")
    steps = width // BLOCK
    own_hl, left_hl, right_hl, back_hl = (jnp.asarray(m) for m in transforms())
    seg = segments.reshape(1, ROWS)
    gain_row = gain.reshape(1, width)
    act = jax.ShapeDtypeStruct((ROWS, width), jnp.bfloat16)

    prod = (k_act.astype(jnp.float32) * v_act.astype(jnp.float32)).astype(jnp.bfloat16)
    in_last = (segments == segments[ROWS - 1]).astype(jnp.bfloat16)
    row = lax.broadcasted_iota(jnp.int32, (ROWS, width), 0)
    message = jnp.where(row == 0, (segments[ROWS - 1] % 2).astype(jnp.bfloat16), prod * in_last[:, None])
    halo = shifted(message, "ctx", 1)

    wide, square = whole((256, 256)), whole((1, ROWS))
    stats_spec = whole((n_hid, 2, ROWS))
    conv, stats = pl.pallas_call(
        conv_kernel,
        grid=(steps,),
        in_specs=[wide, wide, wide, square, columns(ROWS), columns(ROWS), columns(ROWS), columns(ROWS), columns(ROWS), columns(ROWS), columns(1)],
        out_specs=[columns(ROWS), stats_spec],
        out_shape=[jax.ShapeDtypeStruct((ROWS, width), jnp.float32), jax.ShapeDtypeStruct((n_hid, 2, ROWS), jnp.float32)],
        scratch_shapes=[pltpu.VMEM((2, ROWS, ROWS), jnp.float32)],
        compiler_params=params(),
        cost_estimate=cost(8 * 2**27, 3 * 2**20),
        name="conv_stats",
    )(own_hl, left_hl, back_hl, seg, k_act, v_act, halo, filt, q_act, grad_out, gain_row)
    stats = lax.all_to_all(stats, "hid", 0, 0, tiled=True)

    groups = (8, width // ROWS, 9, 2, ROWS)
    chunks, dconv, head = pl.pallas_call(
        grad_kernel,
        grid=(steps,),
        in_specs=[wide, wide, wide, square, columns(ROWS), columns(ROWS), columns(ROWS), columns(ROWS), columns(ROWS), columns(1), columns(ROWS), stats_spec],
        out_specs=[pl.BlockSpec((8, BLOCK // ROWS, 9, 2, ROWS), lambda i: (0, i, 0, 0, 0)), columns(ROWS), columns(ROWS)],
        out_shape=[jax.ShapeDtypeStruct(groups, jnp.bfloat16), act, act],
        compiler_params=params(),
        cost_estimate=cost(8 * 2**27, 3 * 2**20),
        name="filter_grad",
    )(own_hl, left_hl, back_hl, seg, k_act, v_act, halo, q_act, grad_out, gain_row, conv, stats)

    chunks = chunks.reshape(n_ctx, 9, 2, ROWS)
    parts = lax.all_to_all(chunks, "ctx", 0, 0, tiled=True)
    tail = shifted(head, "ctx", -1)

    layer_out, q_grad, k_grad, v_grad = pl.pallas_call(
        out_kernel,
        grid=(steps,),
        in_specs=[wide, wide, wide, square, columns(ROWS), columns(ROWS), columns(ROWS), columns(ROWS), columns(1), columns(ROWS), stats_spec, columns(ROWS), columns(ROWS), columns(ROWS)],
        out_specs=[columns(ROWS)] * 4,
        out_shape=[act] * 4,
        compiler_params=params(),
        cost_estimate=cost(8 * 2**27, 4 * 2**20),
        name="input_grads",
    )(own_hl, right_hl, back_hl, seg, k_act, v_act, q_act, grad_out, gain_row, conv, stats, dconv, tail, filt)

    total = jnp.sum(parts.astype(jnp.float32), axis=0)
    gain_total = total[8, 0] + total[8, 1]
    gain_high = gain_total.astype(jnp.bfloat16)
    gain_low = (gain_total - gain_high.astype(jnp.float32)).astype(jnp.bfloat16)
    mine = jnp.concatenate([total[:8].astype(jnp.bfloat16), jnp.stack([gain_high, gain_low])[None]], axis=0)
    full = lax.all_to_all(jnp.broadcast_to(mine[None], parts.shape), "ctx", 0, 0, tiled=True)
    full = full.reshape(groups)
    filt_grad = full[:, :, :8].transpose(0, 2, 3, 1, 4).reshape(ROWS, width).astype(jnp.float32)
    gain_grad = (full[0, :, 8, 0].astype(jnp.float32) + full[0, :, 8, 1].astype(jnp.float32)).reshape(width)
    return (layer_out, q_grad, k_grad, v_grad, filt_grad, gain_grad)


def solution(mesh):
    in_specs = (
        P("ctx", "hid"),
        P("ctx", "hid"),
        P("ctx", "hid"),
        P(None, "hid"),
        P("hid"),
        P("ctx"),
        P("ctx", "hid"),
    )
    out_specs = (
        P("ctx", "hid"),
        P("ctx", "hid"),
        P("ctx", "hid"),
        P("ctx", "hid"),
        P(None, "hid"),
        P("hid"),
    )
    return jax.shard_map(local, mesh=mesh, in_specs=in_specs, out_specs=out_specs, check_vma=False)
```

```python
import jax
import jax.numpy as jnp
import ml_dtypes
import numpy as np
from jax import lax
from jax.experimental import pallas as pl
from jax.experimental.pallas import tpu as pltpu
from jax.sharding import PartitionSpec as P

C = 8192
ROWS = 128
FREQ = 128
BLOCK = 256


def split_const(matrix):
    high = matrix.astype(ml_dtypes.bfloat16)
    low = (matrix - high.astype(np.float64)).astype(ml_dtypes.bfloat16)
    return high, low


def transforms():
    omega = 2.0 * np.pi * (np.arange(FREQ) + 0.5) / (2 * FREQ)

    def at(positions):
        angle = omega[:, None] * positions[None, :]
        return np.concatenate([np.cos(angle), -np.sin(angle)], axis=0)

    here = np.arange(ROWS)
    own = at(here)
    left = at(here - ROWS)
    left[:, 0] = 0.0
    right = at(here + ROWS)
    right[:, -1] = 0.0
    own_hl = np.concatenate(split_const(own), axis=1)
    left_hl = np.concatenate(split_const(left), axis=1)
    right_hl = np.concatenate(split_const(right), axis=1)
    back_hl = np.concatenate(split_const(own.T / FREQ), axis=0)
    return np.stack([own_hl, back_hl, left_hl, right_hl])


def mm(a, b):
    return jnp.dot(a, b, preferred_element_type=jnp.float32)


def forward(matrix_hl, x):
    return mm(matrix_hl, jnp.concatenate([x, x], axis=0))


def forward_wide(matrix_hl, x):
    high = x.astype(jnp.bfloat16)
    low = (x - high.astype(jnp.float32)).astype(jnp.bfloat16)
    return forward(matrix_hl, high) + mm(matrix_hl[:, :ROWS], low)


def backward(back_hl, spectrum):
    high = spectrum.astype(jnp.bfloat16)
    low = (spectrum - high.astype(jnp.float32)).astype(jnp.bfloat16)
    both = mm(back_hl, high)
    return both[:ROWS] + both[ROWS:] + mm(back_hl[:ROWS], low)


def times(a, b):
    ar, ai, br, bi = a[:FREQ], a[FREQ:], b[:FREQ], b[FREQ:]
    return jnp.concatenate([ar * br - ai * bi, ar * bi + ai * br], axis=0)


def times_conj(a, b):
    ar, ai, br, bi = a[:FREQ], a[FREQ:], b[:FREQ], b[FREQ:]
    return jnp.concatenate([ar * br + ai * bi, ai * br - ar * bi], axis=0)


def down(row, width):
    square = jnp.broadcast_to(row, (ROWS, ROWS)).T
    return jnp.concatenate([square] * (width // ROWS), axis=1)


def first_doc(seg):
    return (seg == seg[:, :1]).astype(jnp.float32)


def last_doc(seg):
    return (seg == seg[:, ROWS - 1 :]).astype(jnp.float32)


def parity(seg):
    return (seg % 2).astype(jnp.float32)


def blocks(width):
    return [slice(i, i + BLOCK) for i in range(0, width, BLOCK)]


def lane_sum(x):
    return sum(x[:, i : i + ROWS] for i in range(0, x.shape[1], ROWS))


def fetch(pairs, sems):
    copies = [pltpu.make_async_copy(source, target, sems.at[i]) for i, (source, target) in enumerate(pairs)]
    for copy in copies:
        copy.start()
    return copies


def message_kernel(seg_hbm, k_hbm, v_hbm, seg_ref, prod_ref, message_ref, k_ref, v_ref, sems):
    parts = blocks(k_ref.shape[1])
    pairs = [(seg_hbm, seg_ref)]
    for at in parts:
        pairs += [(k_hbm.at[:, at], k_ref.at[:, at]), (v_hbm.at[:, at], v_ref.at[:, at])]
    copies = fetch(pairs, sems)
    copies[0].wait()
    seg = seg_ref[...]
    in_last = down(last_doc(seg), BLOCK)
    is_top = lax.broadcasted_iota(jnp.int32, (ROWS, BLOCK), 0) == 0
    mark = parity(seg[:, ROWS - 1 :])
    for i, at in enumerate(parts):
        copies[2 * i + 1].wait()
        copies[2 * i + 2].wait()
        prod = (k_ref[:, at].astype(jnp.float32) * v_ref[:, at].astype(jnp.float32)).astype(jnp.bfloat16)
        prod_ref[:, at] = prod
        message_ref[:, at] = jnp.where(is_top, mark, prod.astype(jnp.float32) * in_last).astype(jnp.bfloat16)


def own_kernel(dft_hbm, filt_hbm, q_hbm, g_hbm, gain_hbm, seg_ref, prod_ref, dft_ref, q_ref, g_ref, gain_ref, taps_ref, all_ref, rest_ref, conv_ref, filt_ref, sems):
    copies = fetch([(dft_hbm, dft_ref), (filt_hbm, filt_ref), (q_hbm, q_ref), (g_hbm, g_ref), (gain_hbm, gain_ref)], sems)
    in_first = down(first_doc(seg_ref[...]), BLOCK)
    outside = (1.0 - in_first).astype(jnp.bfloat16)
    copies[0].wait()
    copies[1].wait()
    own, back = dft_ref[0], dft_ref[1]
    for at in blocks(prod_ref.shape[1]):
        prod = prod_ref[:, at]
        taps = forward_wide(own, filt_ref[:, at])
        all_spec = forward(own, prod)
        rest_spec = forward(own, prod * outside)
        taps_ref[:, at] = taps
        all_ref[:, at] = all_spec
        rest_ref[:, at] = rest_spec
        conv_first = backward(back, times(all_spec, taps))
        conv_rest = backward(back, times(rest_spec, taps))
        conv_ref[:, at] = jnp.where(in_first > 0.5, conv_first, conv_rest)
    for copy in copies[2:]:
        copy.wait()


def halo_kernel(dft_ref, seg_ref, halo_ref, taps_ref, all_ref, own_conv_ref, q_ref, g_ref, gain_ref, conv_ref, spec_ref, stats_ref):
    seg = seg_ref[...]
    in_first = down(first_doc(seg), BLOCK)
    mark = parity(seg[:, :1])
    back, left = dft_ref[1], dft_ref[2]
    square, inner = 0.0, 0.0
    for at in blocks(q_ref.shape[1]):
        halo = halo_ref[:, at]
        joined = (halo[0:1].astype(jnp.float32) == mark).astype(jnp.float32)
        halo_spec = forward(left, halo) * joined
        spec_ref[:, at] = all_ref[:, at] + halo_spec
        conv = own_conv_ref[:, at] + in_first * backward(back, times(halo_spec, taps_ref[:, at]))
        conv_ref[:, at] = conv
        y = q_ref[:, at].astype(jnp.float32) * conv
        square += lane_sum(y * y)
        inner += lane_sum(g_ref[:, at].astype(jnp.float32) * gain_ref[:, at] * y)
    rows = jnp.concatenate([jnp.sum(square.T, axis=0, keepdims=True), jnp.sum(inner.T, axis=0, keepdims=True)], axis=0)
    stats_ref[...] = jnp.broadcast_to(rows[None], stats_ref.shape)


def scales(stats_ref):
    total = jnp.sum(stats_ref[...], axis=0)
    rinv = lax.rsqrt(total[0:1] / C + 1e-06)
    return down(rinv, BLOCK), down(rinv * rinv * rinv * total[1:2] / C, BLOCK)


def filter_kernel(dft_ref, seg_ref, stats_ref, conv_ref, spec_ref, rest_ref, q_ref, g_ref, gain_ref, chunk_ref, head_ref):
    rinv, slope = scales(stats_ref)
    seg = seg_ref[...]
    first = down(first_doc(seg), BLOCK).astype(jnp.bfloat16)
    is_end = lax.broadcasted_iota(jnp.int32, (ROWS, BLOCK), 0) == ROWS - 1
    mark = parity(seg[:, :1])
    own, back = dft_ref[0], dft_ref[1]
    for step, at in enumerate(blocks(q_ref.shape[1])):
        query = q_ref[:, at].astype(jnp.float32)
        up = g_ref[:, at].astype(jnp.float32)
        y = query * conv_ref[:, at]
        dy = rinv * (up * gain_ref[:, at]) - y * slope
        dconv = (dy * query).astype(jnp.bfloat16)
        d_first = dconv * first
        head_ref[:, at] = jnp.where(is_end, mark, d_first.astype(jnp.float32)).astype(jnp.bfloat16)
        first_spec = forward(own, d_first)
        rest_spec = forward(own, dconv - d_first)
        spectrum = times_conj(first_spec, spec_ref[:, at]) + times_conj(rest_spec, rest_ref[:, at])
        taps = backward(back, spectrum).astype(jnp.bfloat16)
        gain_sum = jnp.sum(up * y * rinv, axis=0, keepdims=True)
        gain_high = gain_sum.astype(jnp.bfloat16)
        gain_low = (gain_sum - gain_high.astype(jnp.float32)).astype(jnp.bfloat16)
        gain_both = jnp.concatenate([gain_high, gain_low], axis=0)
        for sub in range(BLOCK // ROWS):
            lanes = slice(sub * ROWS, (sub + 1) * ROWS)
            block = step * (BLOCK // ROWS) + sub
            for group in range(8):
                for pair in range(8):
                    row = group * 16 + pair * 2
                    chunk_ref[group, block, pair] = taps[row : row + 2, lanes]
                chunk_ref[group, block, 8] = gain_both[:, lanes]


def out_kernel(q_hbm, g_hbm, stats_ref, conv_ref, gain_ref, layer_ref, qg_ref, dconv_ref, q_ref, g_ref, sems):
    copies = fetch([(q_hbm, q_ref), (g_hbm, g_ref)], sems)
    rinv, slope = scales(stats_ref)
    for copy in copies:
        copy.wait()
    for at in blocks(q_ref.shape[1]):
        query, conv, gain = q_ref[:, at].astype(jnp.float32), conv_ref[:, at], gain_ref[:, at]
        y = query * conv
        dy = rinv * (g_ref[:, at].astype(jnp.float32) * gain) - y * slope
        layer_ref[:, at] = (y * rinv * gain).astype(jnp.bfloat16)
        qg_ref[:, at] = (dy * conv).astype(jnp.bfloat16)
        dconv_ref[:, at] = (dy * query).astype(jnp.bfloat16)


def input_kernel(k_hbm, v_hbm, dft_ref, seg_ref, dconv_ref, tail_ref, taps_ref, kg_ref, vg_ref, k_ref, v_ref, sems):
    copies = fetch([(k_hbm, k_ref), (v_hbm, v_ref)], sems)
    seg = seg_ref[...]
    in_last = down(last_doc(seg), BLOCK)
    in_first = down(first_doc(seg), BLOCK).astype(jnp.bfloat16)
    mark = parity(seg[:, ROWS - 1 :])
    own, back, right = dft_ref[0], dft_ref[1], dft_ref[3]
    for copy in copies:
        copy.wait()
    for at in blocks(k_ref.shape[1]):
        dconv, tail, taps = dconv_ref[:, at], tail_ref[:, at], taps_ref[:, at]
        joined = (tail[ROWS - 1 :].astype(jnp.float32) == mark).astype(jnp.float32)
        last_spec = forward(own, dconv) + forward(right, tail) * joined
        first_spec = forward(own, dconv * in_first)
        dprod_last = backward(back, times_conj(last_spec, taps))
        dprod_first = backward(back, times_conj(first_spec, taps))
        dprod = jnp.where(in_last > 0.5, dprod_last, dprod_first)
        kg_ref[:, at] = (dprod * v_ref[:, at].astype(jnp.float32)).astype(jnp.bfloat16)
        vg_ref[:, at] = (dprod * k_ref[:, at].astype(jnp.float32)).astype(jnp.bfloat16)


def total_kernel(parts_ref, mine_ref):
    total = jnp.sum(parts_ref[...].astype(jnp.float32), axis=0)
    gain = total[8, 0:1] + total[8, 1:2]
    gain_high = gain.astype(jnp.bfloat16)
    gain_low = (gain - gain_high.astype(jnp.float32)).astype(jnp.bfloat16)
    mine = jnp.concatenate([total[:8].astype(jnp.bfloat16), jnp.concatenate([gain_high, gain_low], axis=0)[None]], axis=0)
    mine_ref[...] = jnp.broadcast_to(mine[None], mine_ref.shape)


def gather_kernel(full_ref, filt_ref, gain_ref):
    for block in range(full_ref.shape[1]):
        lanes = slice(block * ROWS, (block + 1) * ROWS)
        for group in range(8):
            for pair in range(8):
                row = group * 16 + pair * 2
                filt_ref[row : row + 2, lanes] = full_ref[group, block, pair].astype(jnp.float32)
        gain = full_ref[0, block, 8].astype(jnp.float32)
        gain_ref[:, lanes] = gain[0:1] + gain[1:2]


def call(kernel, name, outs, flops, hbm, vmem, scratch=(), pinned=True):
    hbm = [pltpu.with_memory_space_constraint(a, pltpu.HBM) for a in hbm]
    args = (*hbm, *vmem)
    moved = sum(a.size * a.dtype.itemsize for a in args)
    here = pl.BlockSpec(memory_space=pltpu.VMEM)
    space = pltpu.VMEM if pinned else jax.ShapeDtypeStruct
    return pl.pallas_call(
        kernel,
        in_specs=[pl.BlockSpec(memory_space=pltpu.HBM)] * len(hbm) + [here] * len(vmem),
        out_specs=[here] * len(outs),
        out_shape=[space(shape, dtype) for shape, dtype in outs],
        scratch_shapes=scratch,
        compiler_params=pltpu.CompilerParams(vmem_limit_bytes=32 * 1024 * 1024),
        cost_estimate=pl.CostEstimate(flops=flops, bytes_accessed=moved, transcendentals=0),
        name=name,
    )(*args)


def shifted(value, axis, steps):
    count = lax.axis_size(axis)
    first, last = (max(0, -steps), min(count, count - steps))
    return lax.ppermute(value, axis, [(source, source + steps) for source in range(first, last)])


def local(q_act, k_act, v_act, filt, gain, segments, grad_out):
    width = q_act.shape[1]
    n_ctx, n_hid = lax.axis_size("ctx"), lax.axis_size("hid")
    dft = jnp.asarray(transforms())
    seg = segments.reshape(1, ROWS)
    gain_row = gain.reshape(1, width)
    act = ((ROWS, width), jnp.bfloat16)
    wide = ((ROWS, width), jnp.float32)
    spec = ((2 * FREQ, width), jnp.float32)
    unit = 2**27

    row = ((1, width), jnp.float32)
    sems = pltpu.SemaphoreType.DMA((1 + 2 * (width // BLOCK),))
    mine = pltpu.VMEM((ROWS, width), jnp.bfloat16)
    seg, prod, message = call(
        message_kernel, "message", [((1, ROWS), jnp.int32), act, act], 2**18, (seg, k_act, v_act), (), [mine, mine, sems]
    )
    halo = shifted(message, "ctx", 1)
    dft, q_here, g_here, gain_here, taps, all_spec, rest_spec, own_conv = call(
        own_kernel,
        "own_conv",
        [(dft.shape, dft.dtype), act, act, row, spec, spec, spec, wide],
        8 * unit,
        (dft, filt, q_act, grad_out, gain_row),
        (seg, prod),
        [pltpu.VMEM(filt.shape, filt.dtype), pltpu.SemaphoreType.DMA((5,))],
    )
    conv, all_spec, stats = call(
        halo_kernel,
        "halo_conv",
        [wide, spec, ((n_hid, 2, ROWS), jnp.float32)],
        3 * unit,
        (),
        (dft, seg, halo, taps, all_spec, own_conv, q_here, g_here, gain_here),
    )
    stats = lax.all_to_all(stats, "hid", 0, 0, tiled=True)

    groups = (8, width // ROWS, 9, 2, ROWS)
    chunks, head = call(
        filter_kernel,
        "filter_grad",
        [(groups, jnp.bfloat16), act],
        5 * unit,
        (),
        (dft, seg, stats, conv, all_spec, rest_spec, q_here, g_here, gain_here),
    )
    parts = lax.all_to_all(chunks.reshape(n_ctx, 9, 2, ROWS), "ctx", 0, 0, tiled=True)
    parts, head = lax.optimization_barrier((parts, head))
    (total,) = call(total_kernel, "total", [(parts.shape, parts.dtype)], 2**18, (), (parts,))
    full = lax.all_to_all(total, "ctx", 0, 0, tiled=True)
    tail = shifted(head, "ctx", -1)
    pair = [mine, mine, pltpu.SemaphoreType.DMA((2,))]
    layer_out, q_grad, dconv = call(
        out_kernel, "out_grads", [act] * 3, 2**20, (q_act, grad_out), (stats, conv, gain_here), pair, False
    )
    k_grad, v_grad = call(
        input_kernel, "input_grads", [act, act], 6 * unit, (k_act, v_act), (dft, seg, dconv, tail, taps), pair, False
    )
    filt_grad, gain_grad = call(
        gather_kernel, "gather", [wide, row], 2**18, (), (full.reshape(groups),), (), False
    )
    return (layer_out, q_grad, k_grad, v_grad, filt_grad, gain_grad.reshape(width))


def solution(mesh):
    in_specs = (
        P("ctx", "hid"),
        P("ctx", "hid"),
        P("ctx", "hid"),
        P(None, "hid"),
        P("hid"),
        P("ctx"),
        P("ctx", "hid"),
    )
    out_specs = (
        P("ctx", "hid"),
        P("ctx", "hid"),
        P("ctx", "hid"),
        P("ctx", "hid"),
        P(None, "hid"),
        P("hid"),
    )
    return jax.shard_map(local, mesh=mesh, in_specs=in_specs, out_specs=out_specs, check_vma=False)
```

```python
import jax
import jax.numpy as jnp
import ml_dtypes
import numpy as np
from jax import lax
from jax.experimental import pallas as pl
from jax.experimental.pallas import tpu as pltpu
from jax.sharding import PartitionSpec as P

C = 8192
ROWS = 128
FREQ = 128
BLOCK = 256


def split_const(matrix):
    high = matrix.astype(ml_dtypes.bfloat16)
    low = (matrix - high.astype(np.float64)).astype(ml_dtypes.bfloat16)
    return high, low


def transforms():
    omega = 2.0 * np.pi * (np.arange(FREQ) + 0.5) / (2 * FREQ)

    def at(positions):
        angle = omega[:, None] * positions[None, :]
        return np.concatenate([np.cos(angle), -np.sin(angle)], axis=0)

    here = np.arange(ROWS)
    own = at(here)
    left = at(here - ROWS)
    left[:, 0] = 0.0
    right = at(here + ROWS)
    right[:, -1] = 0.0
    own_hl = np.concatenate(split_const(own), axis=1)
    left_hl = np.concatenate(split_const(left), axis=1)
    right_hl = np.concatenate(split_const(right), axis=1)
    back_hl = np.concatenate(split_const(own.T / FREQ), axis=0)
    return np.stack([own_hl, back_hl, left_hl, right_hl])


def mm(a, b):
    return jnp.dot(a, b, preferred_element_type=jnp.float32)


def forward(matrix_hl, x):
    return mm(matrix_hl, jnp.concatenate([x, x], axis=0))


def forward_wide(matrix_hl, x):
    high = x.astype(jnp.bfloat16)
    low = (x - high.astype(jnp.float32)).astype(jnp.bfloat16)
    return forward(matrix_hl, high) + mm(matrix_hl[:, :ROWS], low)


def backward(back_hl, spectrum):
    high = spectrum.astype(jnp.bfloat16)
    low = (spectrum - high.astype(jnp.float32)).astype(jnp.bfloat16)
    both = mm(back_hl, high)
    return both[:ROWS] + both[ROWS:] + mm(back_hl[:ROWS], low)


def times(a, b):
    ar, ai, br, bi = a[:FREQ], a[FREQ:], b[:FREQ], b[FREQ:]
    return jnp.concatenate([ar * br - ai * bi, ar * bi + ai * br], axis=0)


def times_conj(a, b):
    ar, ai, br, bi = a[:FREQ], a[FREQ:], b[:FREQ], b[FREQ:]
    return jnp.concatenate([ar * br + ai * bi, ai * br - ar * bi], axis=0)


def down(row, width):
    square = jnp.broadcast_to(row, (ROWS, ROWS)).T
    return jnp.concatenate([square] * (width // ROWS), axis=1)


def first_doc(seg):
    return (seg == seg[:, :1]).astype(jnp.float32)


def last_doc(seg):
    return (seg == seg[:, ROWS - 1 :]).astype(jnp.float32)


def parity(seg):
    return (seg % 2).astype(jnp.float32)


def blocks(width):
    return [slice(i, i + BLOCK) for i in range(0, width, BLOCK)]


def lane_sum(x):
    return sum(x[:, i : i + ROWS] for i in range(0, x.shape[1], ROWS))


def fetch(pairs, sems):
    copies = [pltpu.make_async_copy(source, target, sems.at[i]) for i, (source, target) in enumerate(pairs)]
    for copy in copies:
        copy.start()
    return copies


def message_kernel(seg_hbm, k_hbm, v_hbm, seg_ref, prod_ref, message_ref, k_ref, v_ref, sems):
    parts = blocks(k_ref.shape[1])
    pairs = [(seg_hbm, seg_ref)]
    for at in parts:
        pairs += [(k_hbm.at[:, at], k_ref.at[:, at]), (v_hbm.at[:, at], v_ref.at[:, at])]
    copies = fetch(pairs, sems)
    copies[0].wait()
    seg = seg_ref[...]
    in_last = down(last_doc(seg), BLOCK)
    is_top = lax.broadcasted_iota(jnp.int32, (ROWS, BLOCK), 0) == 0
    mark = parity(seg[:, ROWS - 1 :])
    for i, at in enumerate(parts):
        copies[2 * i + 1].wait()
        copies[2 * i + 2].wait()
        prod = (k_ref[:, at].astype(jnp.float32) * v_ref[:, at].astype(jnp.float32)).astype(jnp.bfloat16)
        prod_ref[:, at] = prod
        message_ref[:, at] = jnp.where(is_top, mark, prod.astype(jnp.float32) * in_last).astype(jnp.bfloat16)


def own_kernel(dft_hbm, filt_hbm, q_hbm, g_hbm, gain_hbm, seg_ref, prod_ref, dft_ref, q_ref, g_ref, gain_ref, taps_ref, all_ref, rest_ref, conv_ref, filt_ref, sems):
    copies = fetch([(dft_hbm, dft_ref), (filt_hbm, filt_ref), (q_hbm, q_ref), (g_hbm, g_ref), (gain_hbm, gain_ref)], sems)
    in_first = down(first_doc(seg_ref[...]), BLOCK)
    outside = (1.0 - in_first).astype(jnp.bfloat16)
    copies[0].wait()
    copies[1].wait()
    own, back = dft_ref[0], dft_ref[1]
    for at in blocks(prod_ref.shape[1]):
        prod = prod_ref[:, at]
        taps = forward_wide(own, filt_ref[:, at])
        all_spec = forward(own, prod)
        rest_spec = forward(own, prod * outside)
        taps_ref[:, at] = taps
        all_ref[:, at] = all_spec
        rest_ref[:, at] = rest_spec
        conv_first = backward(back, times(all_spec, taps))
        conv_rest = backward(back, times(rest_spec, taps))
        conv_ref[:, at] = jnp.where(in_first > 0.5, conv_first, conv_rest)
    for copy in copies[2:]:
        copy.wait()


def halo_kernel(dft_ref, seg_ref, halo_ref, taps_ref, all_ref, own_conv_ref, q_ref, g_ref, gain_ref, conv_ref, spec_ref, stats_ref):
    seg = seg_ref[...]
    in_first = down(first_doc(seg), BLOCK)
    mark = parity(seg[:, :1])
    back, left = dft_ref[1], dft_ref[2]
    square, inner = 0.0, 0.0
    for at in blocks(q_ref.shape[1]):
        halo = halo_ref[:, at]
        joined = (halo[0:1].astype(jnp.float32) == mark).astype(jnp.float32)
        halo_spec = forward(left, halo) * joined
        spec_ref[:, at] = all_ref[:, at] + halo_spec
        conv = own_conv_ref[:, at] + in_first * backward(back, times(halo_spec, taps_ref[:, at]))
        conv_ref[:, at] = conv
        y = q_ref[:, at].astype(jnp.float32) * conv
        square += lane_sum(y * y)
        inner += lane_sum(g_ref[:, at].astype(jnp.float32) * gain_ref[:, at] * y)
    rows = jnp.concatenate([jnp.sum(square.T, axis=0, keepdims=True), jnp.sum(inner.T, axis=0, keepdims=True)], axis=0)
    stats_ref[...] = jnp.broadcast_to(rows[None], stats_ref.shape)


def scales(stats_ref):
    total = jnp.sum(stats_ref[...], axis=0)
    rinv = lax.rsqrt(total[0:1] / C + 1e-06)
    return down(rinv, BLOCK), down(rinv * rinv * rinv * total[1:2] / C, BLOCK)


def filter_kernel(dft_ref, seg_ref, stats_ref, conv_ref, spec_ref, rest_ref, q_ref, g_ref, gain_ref, chunk_ref, head_ref):
    rinv, slope = scales(stats_ref)
    seg = seg_ref[...]
    first = down(first_doc(seg), BLOCK).astype(jnp.bfloat16)
    is_end = lax.broadcasted_iota(jnp.int32, (ROWS, BLOCK), 0) == ROWS - 1
    mark = parity(seg[:, :1])
    own, back = dft_ref[0], dft_ref[1]
    for step, at in enumerate(blocks(q_ref.shape[1])):
        query = q_ref[:, at].astype(jnp.float32)
        up = g_ref[:, at].astype(jnp.float32)
        y = query * conv_ref[:, at]
        dy = rinv * (up * gain_ref[:, at]) - y * slope
        dconv = (dy * query).astype(jnp.bfloat16)
        d_first = dconv * first
        head_ref[:, at] = jnp.where(is_end, mark, d_first.astype(jnp.float32)).astype(jnp.bfloat16)
        first_spec = forward(own, d_first)
        rest_spec = forward(own, dconv - d_first)
        spectrum = times_conj(first_spec, spec_ref[:, at]) + times_conj(rest_spec, rest_ref[:, at])
        taps = backward(back, spectrum).astype(jnp.bfloat16)
        gain_sum = jnp.sum(up * y * rinv, axis=0, keepdims=True)
        gain_high = gain_sum.astype(jnp.bfloat16)
        gain_low = (gain_sum - gain_high.astype(jnp.float32)).astype(jnp.bfloat16)
        gain_both = jnp.concatenate([gain_high, gain_low], axis=0)
        for sub in range(BLOCK // ROWS):
            lanes = slice(sub * ROWS, (sub + 1) * ROWS)
            block = step * (BLOCK // ROWS) + sub
            for group in range(8):
                for pair in range(8):
                    row = group * 16 + pair * 2
                    chunk_ref[group, block, pair] = taps[row : row + 2, lanes]
                chunk_ref[group, block, 8] = gain_both[:, lanes]


def out_kernel(q_hbm, g_hbm, k_hbm, v_hbm, dft_ref, seg_ref, stats_ref, conv_ref, taps_ref, gain_ref, layer_ref, qg_ref, dprod_ref, k_ref, v_ref, q_ref, g_ref, sems):
    copies = fetch([(q_hbm, q_ref), (g_hbm, g_ref), (k_hbm, k_ref), (v_hbm, v_ref)], sems)
    rinv, slope = scales(stats_ref)
    seg = seg_ref[...]
    in_last = down(last_doc(seg), BLOCK)
    in_first = down(first_doc(seg), BLOCK).astype(jnp.bfloat16)
    own, back = dft_ref[0], dft_ref[1]
    copies[0].wait()
    copies[1].wait()
    for at in blocks(q_ref.shape[1]):
        query, conv, gain = q_ref[:, at].astype(jnp.float32), conv_ref[:, at], gain_ref[:, at]
        y = query * conv
        dy = rinv * (g_ref[:, at].astype(jnp.float32) * gain) - y * slope
        layer_ref[:, at] = (y * rinv * gain).astype(jnp.bfloat16)
        qg_ref[:, at] = (dy * conv).astype(jnp.bfloat16)
        dconv = (dy * query).astype(jnp.bfloat16)
        taps = taps_ref[:, at]
        dprod_last = backward(back, times_conj(forward(own, dconv), taps))
        dprod_first = backward(back, times_conj(forward(own, dconv * in_first), taps))
        dprod_ref[:, at] = jnp.where(in_last > 0.5, dprod_last, dprod_first)
    copies[2].wait()
    copies[3].wait()


def input_kernel(dft_ref, seg_ref, dprod_ref, tail_ref, taps_ref, k_ref, v_ref, kg_ref, vg_ref):
    seg = seg_ref[...]
    in_last = down(last_doc(seg), BLOCK)
    mark = parity(seg[:, ROWS - 1 :])
    back, right = dft_ref[1], dft_ref[3]
    for at in blocks(k_ref.shape[1]):
        tail = tail_ref[:, at]
        joined = (tail[ROWS - 1 :].astype(jnp.float32) == mark).astype(jnp.float32)
        tail_spec = forward(right, tail) * joined
        dprod = dprod_ref[:, at] + in_last * backward(back, times_conj(tail_spec, taps_ref[:, at]))
        kg_ref[:, at] = (dprod * v_ref[:, at].astype(jnp.float32)).astype(jnp.bfloat16)
        vg_ref[:, at] = (dprod * k_ref[:, at].astype(jnp.float32)).astype(jnp.bfloat16)


def total_kernel(parts_ref, mine_ref):
    total = jnp.sum(parts_ref[...].astype(jnp.float32), axis=0)
    gain = total[8, 0:1] + total[8, 1:2]
    gain_high = gain.astype(jnp.bfloat16)
    gain_low = (gain - gain_high.astype(jnp.float32)).astype(jnp.bfloat16)
    mine = jnp.concatenate([total[:8].astype(jnp.bfloat16), jnp.concatenate([gain_high, gain_low], axis=0)[None]], axis=0)
    mine_ref[...] = jnp.broadcast_to(mine[None], mine_ref.shape)


def gather_kernel(full_ref, filt_ref, gain_ref):
    for block in range(full_ref.shape[1]):
        lanes = slice(block * ROWS, (block + 1) * ROWS)
        for group in range(8):
            for pair in range(8):
                row = group * 16 + pair * 2
                filt_ref[row : row + 2, lanes] = full_ref[group, block, pair].astype(jnp.float32)
        gain = full_ref[0, block, 8].astype(jnp.float32)
        gain_ref[:, lanes] = gain[0:1] + gain[1:2]


def call(kernel, name, outs, flops, hbm, vmem, scratch=(), pinned=True):
    hbm = [pltpu.with_memory_space_constraint(a, pltpu.HBM) for a in hbm]
    args = (*hbm, *vmem)
    moved = sum(a.size * a.dtype.itemsize for a in args)
    here = pl.BlockSpec(memory_space=pltpu.VMEM)
    space = pltpu.VMEM if pinned else jax.ShapeDtypeStruct
    return pl.pallas_call(
        kernel,
        in_specs=[pl.BlockSpec(memory_space=pltpu.HBM)] * len(hbm) + [here] * len(vmem),
        out_specs=[here] * len(outs),
        out_shape=[space(shape, dtype) for shape, dtype in outs],
        scratch_shapes=scratch,
        compiler_params=pltpu.CompilerParams(vmem_limit_bytes=32 * 1024 * 1024),
        cost_estimate=pl.CostEstimate(flops=flops, bytes_accessed=moved, transcendentals=0),
        name=name,
    )(*args)


def shifted(value, axis, steps):
    count = lax.axis_size(axis)
    first, last = (max(0, -steps), min(count, count - steps))
    return lax.ppermute(value, axis, [(source, source + steps) for source in range(first, last)])


def local(q_act, k_act, v_act, filt, gain, segments, grad_out):
    width = q_act.shape[1]
    n_ctx, n_hid = lax.axis_size("ctx"), lax.axis_size("hid")
    dft = jnp.asarray(transforms())
    seg = segments.reshape(1, ROWS)
    gain_row = gain.reshape(1, width)
    act = ((ROWS, width), jnp.bfloat16)
    wide = ((ROWS, width), jnp.float32)
    spec = ((2 * FREQ, width), jnp.float32)
    unit = 2**27

    row = ((1, width), jnp.float32)
    sems = pltpu.SemaphoreType.DMA((1 + 2 * (width // BLOCK),))
    mine = pltpu.VMEM((ROWS, width), jnp.bfloat16)
    seg, prod, message = call(
        message_kernel, "message", [((1, ROWS), jnp.int32), act, act], 2**18, (seg, k_act, v_act), (), [mine, mine, sems]
    )
    halo = shifted(message, "ctx", 1)
    dft, q_here, g_here, gain_here, taps, all_spec, rest_spec, own_conv = call(
        own_kernel,
        "own_conv",
        [(dft.shape, dft.dtype), act, act, row, spec, spec, spec, wide],
        8 * unit,
        (dft, filt, q_act, grad_out, gain_row),
        (seg, prod),
        [pltpu.VMEM(filt.shape, filt.dtype), pltpu.SemaphoreType.DMA((5,))],
    )
    conv, all_spec, stats = call(
        halo_kernel,
        "halo_conv",
        [wide, spec, ((n_hid, 2, ROWS), jnp.float32)],
        3 * unit,
        (),
        (dft, seg, halo, taps, all_spec, own_conv, q_here, g_here, gain_here),
    )
    stats = lax.all_to_all(stats, "hid", 0, 0, tiled=True)

    groups = (8, width // ROWS, 9, 2, ROWS)
    chunks, head = call(
        filter_kernel,
        "filter_grad",
        [(groups, jnp.bfloat16), act],
        5 * unit,
        (),
        (dft, seg, stats, conv, all_spec, rest_spec, q_here, g_here, gain_here),
    )
    parts = lax.all_to_all(chunks.reshape(n_ctx, 9, 2, ROWS), "ctx", 0, 0, tiled=True)
    parts, head = lax.optimization_barrier((parts, head))
    (total,) = call(total_kernel, "total", [(parts.shape, parts.dtype)], 2**18, (), (parts,))
    full = lax.all_to_all(total, "ctx", 0, 0, tiled=True)
    tail = shifted(head, "ctx", -1)
    layer_out, q_grad, own_dprod, k_here, v_here = call(
        out_kernel,
        "out_grads",
        [act, act, wide, act, act],
        6 * unit,
        (q_act, grad_out, k_act, v_act),
        (dft, seg, stats, conv, taps, gain_here),
        [mine, mine, pltpu.SemaphoreType.DMA((4,))],
        False,
    )
    k_grad, v_grad = call(
        input_kernel, "input_grads", [act, act], 3 * unit, (), (dft, seg, own_dprod, tail, taps, k_here, v_here), (), False
    )
    filt_grad, gain_grad = call(
        gather_kernel, "gather", [wide, row], 2**18, (), (full.reshape(groups),), (), False
    )
    return (layer_out, q_grad, k_grad, v_grad, filt_grad, gain_grad.reshape(width))


def solution(mesh):
    in_specs = (
        P("ctx", "hid"),
        P("ctx", "hid"),
        P("ctx", "hid"),
        P(None, "hid"),
        P("hid"),
        P("ctx"),
        P("ctx", "hid"),
    )
    out_specs = (
        P("ctx", "hid"),
        P("ctx", "hid"),
        P("ctx", "hid"),
        P("ctx", "hid"),
        P(None, "hid"),
        P("hid"),
    )
    return jax.shard_map(local, mesh=mesh, in_specs=in_specs, out_specs=out_specs, check_vma=False)
```

```python
import jax
import jax.numpy as jnp
import ml_dtypes
import numpy as np
from jax import lax
from jax.experimental import pallas as pl
from jax.experimental.pallas import tpu as pltpu
from jax.sharding import Mesh
from jax.sharding import PartitionSpec as P

C = 8192
ROWS = 128
FREQ = 128
BLOCK = 1024
PART = 512
COPIES = 4
RUN = 8
HID = ("x", "z_hi")


def split_const(matrix):
    high = matrix.astype(ml_dtypes.bfloat16)
    low = (matrix - high.astype(np.float64)).astype(ml_dtypes.bfloat16)
    return high, low


def transforms():
    omega = 2.0 * np.pi * (np.arange(FREQ) + 0.5) / (2 * FREQ)

    def at(positions):
        angle = omega[:, None] * positions[None, :]
        return np.concatenate([np.cos(angle), -np.sin(angle)], axis=0)

    here = np.arange(ROWS)
    own = at(here)
    left = at(here - ROWS)
    left[:, 0] = 0.0
    right = at(here + ROWS)
    right[:, -1] = 0.0
    own_hl = np.concatenate(split_const(own), axis=1)
    left_hl = np.concatenate(split_const(left), axis=1)
    right_hl = np.concatenate(split_const(right), axis=1)
    back_hl = np.concatenate(split_const(own.T / FREQ), axis=0)
    return np.stack([own_hl, back_hl, left_hl, right_hl])


def mm(a, b):
    return jnp.dot(a, b, preferred_element_type=jnp.float32)


def forward(matrix_hl, x):
    return mm(matrix_hl, jnp.concatenate([x, x], axis=0))


def forward_wide(matrix_hl, x):
    high = x.astype(jnp.bfloat16)
    low = (x - high.astype(jnp.float32)).astype(jnp.bfloat16)
    return forward(matrix_hl, high) + mm(matrix_hl[:, :ROWS], low)


def backward(back_hl, spectrum):
    high = spectrum.astype(jnp.bfloat16)
    low = (spectrum - high.astype(jnp.float32)).astype(jnp.bfloat16)
    both = mm(back_hl, high)
    return both[:ROWS] + both[ROWS:] + mm(back_hl[:ROWS], low)


def times(a, b):
    ar, ai, br, bi = a[:FREQ], a[FREQ:], b[:FREQ], b[FREQ:]
    return jnp.concatenate([ar * br - ai * bi, ar * bi + ai * br], axis=0)


def times_conj(a, b):
    ar, ai, br, bi = a[:FREQ], a[FREQ:], b[:FREQ], b[FREQ:]
    return jnp.concatenate([ar * br + ai * bi, ai * br - ar * bi], axis=0)


def down(row, width):
    square = jnp.broadcast_to(row, (ROWS, ROWS)).T
    return jnp.concatenate([square] * (width // ROWS), axis=1)


def first_doc(seg):
    return (seg == seg[:, :1]).astype(jnp.float32)


def last_doc(seg):
    return (seg == seg[:, ROWS - 1 :]).astype(jnp.float32)


def parity(seg):
    return (seg % 2).astype(jnp.float32)


def blocks(width, size=BLOCK):
    return [slice(i, i + size) for i in range(0, width, size)]


def lane_sum(x):
    return sum(x[:, i : i + ROWS] for i in range(0, x.shape[1], ROWS))


def fetch(pairs, sems):
    copies = [pltpu.make_async_copy(source, target, sems.at[i]) for i, (source, target) in enumerate(pairs)]
    for copy in copies:
        copy.start()
    return copies


def compose(seg_hbm, k_hbm, v_hbm, seg_ref, prod_ref, message_ref, k_ref, v_ref, sems):
    parts = blocks(k_ref.shape[1], PART)
    pairs = [(seg_hbm, seg_ref)]
    for at in parts:
        pairs += [(k_hbm.at[:, at], k_ref.at[:, at]), (v_hbm.at[:, at], v_ref.at[:, at])]
    copies = fetch(pairs, sems)
    copies[0].wait()
    seg = seg_ref[...]
    in_last = down(last_doc(seg), PART)
    is_top = lax.broadcasted_iota(jnp.int32, (ROWS, PART), 0) == 0
    mark = parity(seg[:, ROWS - 1 :])
    for i, at in enumerate(parts):
        copies[2 * i + 1].wait()
        copies[2 * i + 2].wait()
        prod = (k_ref[:, at].astype(jnp.float32) * v_ref[:, at].astype(jnp.float32)).astype(jnp.bfloat16)
        if prod_ref is not None:
            prod_ref[:, at] = prod
        message_ref[:, at] = jnp.where(is_top, mark, prod.astype(jnp.float32) * in_last).astype(jnp.bfloat16)


def far_kernel(seg_hbm, k_hbm, v_hbm, message_ref, seg_ref, k_ref, v_ref, sems):
    @pl.when(lax.axis_index("ctx") % RUN == RUN - 1)
    def _():
        compose(seg_hbm, k_hbm, v_hbm, seg_ref, None, message_ref, k_ref, v_ref, sems)


def message_kernel(seg_hbm, k_hbm, v_hbm, seg_ref, prod_ref, message_ref, k_ref, v_ref, sems):
    compose(seg_hbm, k_hbm, v_hbm, seg_ref, prod_ref, message_ref, k_ref, v_ref, sems)


def own_kernel(dft_hbm, filt_hbm, q_hbm, g_hbm, gain_hbm, seg_ref, prod_ref, dft_ref, q_ref, g_ref, gain_ref, taps_ref, all_ref, rest_ref, conv_ref, filt_ref, sems):
    copies = fetch([(dft_hbm, dft_ref), (filt_hbm, filt_ref), (q_hbm, q_ref), (g_hbm, g_ref), (gain_hbm, gain_ref)], sems)
    in_first = down(first_doc(seg_ref[...]), BLOCK)
    outside = (1.0 - in_first).astype(jnp.bfloat16)
    copies[0].wait()
    copies[1].wait()
    own, back = dft_ref[0], dft_ref[1]
    for at in blocks(prod_ref.shape[1]):
        prod = prod_ref[:, at]
        taps = forward_wide(own, filt_ref[:, at])
        all_spec = forward(own, prod)
        rest_spec = forward(own, prod * outside)
        taps_ref[:, at] = taps
        all_ref[:, at] = all_spec
        rest_ref[:, at] = rest_spec
        conv_first = backward(back, times(all_spec, taps))
        conv_rest = backward(back, times(rest_spec, taps))
        conv_ref[:, at] = jnp.where(in_first > 0.5, conv_first, conv_rest)
    for copy in copies[2:]:
        copy.wait()


def halo_kernel(dft_ref, seg_ref, near_ref, far_ref, taps_ref, all_ref, own_conv_ref, q_ref, g_ref, gain_ref, conv_ref, spec_ref, stats_ref):
    seg = seg_ref[...]
    in_first = down(first_doc(seg), BLOCK)
    mark = parity(seg[:, :1])
    back, left = dft_ref[1], dft_ref[2]
    square, inner = 0.0, 0.0
    for at in blocks(q_ref.shape[1]):
        halo = near_ref[:, at] + far_ref[:, at]
        joined = (halo[0:1].astype(jnp.float32) == mark).astype(jnp.float32)
        halo_spec = forward(left, halo) * joined
        spec_ref[:, at] = all_ref[:, at] + halo_spec
        conv = own_conv_ref[:, at] + in_first * backward(back, times(halo_spec, taps_ref[:, at]))
        conv_ref[:, at] = conv
        y = q_ref[:, at].astype(jnp.float32) * conv
        square += lane_sum(y * y)
        inner += lane_sum(g_ref[:, at].astype(jnp.float32) * gain_ref[:, at] * y)
    rows = jnp.concatenate([jnp.sum(square.T, axis=0, keepdims=True), jnp.sum(inner.T, axis=0, keepdims=True)], axis=0)
    stats_ref[...] = jnp.broadcast_to(rows[None], stats_ref.shape)


def scales(here_ref, there_ref):
    total = jnp.sum(here_ref[...], axis=0) + jnp.sum(there_ref[...], axis=0)
    rinv = lax.rsqrt(total[0:1] / C + 1e-06)
    return down(rinv, BLOCK), down(rinv * rinv * rinv * total[1:2] / C, BLOCK)


def filter_kernel(dft_ref, seg_ref, here_ref, there_ref, conv_ref, spec_ref, rest_ref, q_ref, g_ref, gain_ref, chunk_ref, head_ref):
    rinv, slope = scales(here_ref, there_ref)
    seg = seg_ref[...]
    first = down(first_doc(seg), BLOCK).astype(jnp.bfloat16)
    is_end = lax.broadcasted_iota(jnp.int32, (ROWS, BLOCK), 0) == ROWS - 1
    mark = parity(seg[:, :1])
    own, back = dft_ref[0], dft_ref[1]
    for step, at in enumerate(blocks(q_ref.shape[1])):
        query = q_ref[:, at].astype(jnp.float32)
        up = g_ref[:, at].astype(jnp.float32)
        y = query * conv_ref[:, at]
        dy = rinv * (up * gain_ref[:, at]) - y * slope
        dconv = (dy * query).astype(jnp.bfloat16)
        d_first = dconv * first
        head_ref[:, at] = jnp.where(is_end, mark, d_first.astype(jnp.float32)).astype(jnp.bfloat16)
        first_spec = forward(own, d_first)
        rest_spec = forward(own, dconv - d_first)
        spectrum = times_conj(first_spec, spec_ref[:, at]) + times_conj(rest_spec, rest_ref[:, at])
        taps = backward(back, spectrum).astype(jnp.bfloat16)
        gain_sum = jnp.sum(up * y * rinv, axis=0, keepdims=True)
        gain_high = gain_sum.astype(jnp.bfloat16)
        gain_low = (gain_sum - gain_high.astype(jnp.float32)).astype(jnp.bfloat16)
        gain_both = jnp.concatenate([gain_high, gain_low], axis=0)
        for sub in range(BLOCK // ROWS):
            lanes = slice(sub * ROWS, (sub + 1) * ROWS)
            block = step * (BLOCK // ROWS) + sub
            for group in range(8):
                for pair in range(8):
                    row = group * 16 + pair * 2
                    chunk_ref[group, block, pair] = taps[row : row + 2, lanes]
                chunk_ref[group, block, 8] = gain_both[:, lanes]


def out_kernel(q_hbm, g_hbm, k_hbm, v_hbm, dft_ref, seg_ref, here_ref, there_ref, conv_ref, taps_ref, gain_ref, layer_ref, qg_ref, dprod_ref, k_ref, v_ref, q_ref, g_ref, sems):
    copies = fetch([(q_hbm, q_ref), (g_hbm, g_ref), (k_hbm, k_ref), (v_hbm, v_ref)], sems)
    rinv, slope = scales(here_ref, there_ref)
    seg = seg_ref[...]
    in_last = down(last_doc(seg), BLOCK)
    in_first = down(first_doc(seg), BLOCK).astype(jnp.bfloat16)
    own, back = dft_ref[0], dft_ref[1]
    copies[0].wait()
    copies[1].wait()
    for at in blocks(q_ref.shape[1]):
        query, conv, gain = q_ref[:, at].astype(jnp.float32), conv_ref[:, at], gain_ref[:, at]
        y = query * conv
        dy = rinv * (g_ref[:, at].astype(jnp.float32) * gain) - y * slope
        layer_ref[:, at] = (y * rinv * gain).astype(jnp.bfloat16)
        qg_ref[:, at] = (dy * conv).astype(jnp.bfloat16)
        dconv = (dy * query).astype(jnp.bfloat16)
        taps = taps_ref[:, at]
        dprod_last = backward(back, times_conj(forward(own, dconv), taps))
        dprod_first = backward(back, times_conj(forward(own, dconv * in_first), taps))
        dprod_ref[:, at] = jnp.where(in_last > 0.5, dprod_last, dprod_first)
    copies[2].wait()
    copies[3].wait()


def input_kernel(dft_ref, seg_ref, dprod_ref, tail_ref, taps_ref, k_ref, v_ref, kg_ref, vg_ref):
    seg = seg_ref[...]
    in_last = down(last_doc(seg), BLOCK)
    mark = parity(seg[:, ROWS - 1 :])
    back, right = dft_ref[1], dft_ref[3]
    for at in blocks(k_ref.shape[1]):
        tail = tail_ref[:, at]
        joined = (tail[ROWS - 1 :].astype(jnp.float32) == mark).astype(jnp.float32)
        tail_spec = forward(right, tail) * joined
        dprod = dprod_ref[:, at] + in_last * backward(back, times_conj(tail_spec, taps_ref[:, at]))
        kg_ref[:, at] = (dprod * v_ref[:, at].astype(jnp.float32)).astype(jnp.bfloat16)
        vg_ref[:, at] = (dprod * k_ref[:, at].astype(jnp.float32)).astype(jnp.bfloat16)


def total_kernel(parts_ref, mine_hbm, mine_ref, sems):
    total = jnp.sum(parts_ref[...].astype(jnp.float32), axis=0)
    gain = total[8, 0:1] + total[8, 1:2]
    gain_high = gain.astype(jnp.bfloat16)
    gain_low = (gain - gain_high.astype(jnp.float32)).astype(jnp.bfloat16)
    mine = jnp.concatenate([total[:8].astype(jnp.bfloat16), jnp.concatenate([gain_high, gain_low], axis=0)[None]], axis=0)
    mine_ref[...] = jnp.broadcast_to(mine[None], mine_ref.shape)
    some = mine_ref.shape[0]
    copies = fetch([(mine_ref, mine_hbm.at[pl.ds(i, some)]) for i in range(0, parts_ref.shape[0], some)], sems)
    for copy in copies:
        copy.wait()


def gather_kernel(full_ref, filt_ref, gain_ref):
    for block in range(full_ref.shape[1]):
        lanes = slice(block * ROWS, (block + 1) * ROWS)
        for group in range(8):
            for pair in range(8):
                row = group * 16 + pair * 2
                filt_ref[row : row + 2, lanes] = full_ref[group, block, pair].astype(jnp.float32)
        gain = full_ref[0, block, 8].astype(jnp.float32)
        gain_ref[:, lanes] = gain[0:1] + gain[1:2]


def call(kernel, name, outs, flops, hbm, vmem, scratch=(), pinned=True, sent=0):
    hbm = [pltpu.with_memory_space_constraint(a, pltpu.HBM) for a in hbm]
    args = (*hbm, *vmem)
    moved = sum(a.size * a.dtype.itemsize for a in args)
    here = pl.BlockSpec(memory_space=pltpu.VMEM)
    space = pltpu.VMEM if pinned else jax.ShapeDtypeStruct
    return pl.pallas_call(
        kernel,
        in_specs=[pl.BlockSpec(memory_space=pltpu.HBM)] * len(hbm) + [here] * len(vmem),
        out_specs=[pl.BlockSpec(memory_space=pltpu.HBM)] * sent + [here] * (len(outs) - sent),
        out_shape=[space(shape, dtype) for shape, dtype in outs],
        scratch_shapes=scratch,
        compiler_params=pltpu.CompilerParams(vmem_limit_bytes=32 * 1024 * 1024),
        cost_estimate=pl.CostEstimate(flops=flops, bytes_accessed=moved, transcendentals=0),
        name=name,
    )(*args)


def local(q_act, k_act, v_act, filt, gain, segments, grad_out):
    width = q_act.shape[1]
    n_ctx, n_x = lax.axis_size("ctx"), lax.axis_size("x")
    dft = jnp.asarray(transforms())
    seg = segments.reshape(1, ROWS)
    gain_row = gain.reshape(1, width)
    act = ((ROWS, width), jnp.bfloat16)
    wide = ((ROWS, width), jnp.float32)
    spec = ((2 * FREQ, width), jnp.float32)
    unit = 2**27

    row = ((1, width), jnp.float32)
    sems = pltpu.SemaphoreType.DMA((1 + 2 * (width // PART),))
    mine = pltpu.VMEM((ROWS, width), jnp.bfloat16)
    (far,) = call(
        far_kernel, "far_message", [act], 2**18, (seg, k_act, v_act), (), [pltpu.VMEM((1, ROWS), jnp.int32), mine, mine, sems]
    )
    seg, prod, message = call(
        message_kernel, "message", [((1, ROWS), jnp.int32), act, act], 2**18, (seg, k_act, v_act), (), [mine, mine, sems]
    )
    edges = [(source, source + 1) for source in range(n_ctx - 1)]
    far_halo = lax.ppermute(far, "ctx", [edge for edge in edges if edge[1] % RUN == 0])
    halo = lax.ppermute(message, "ctx", [edge for edge in edges if edge[1] % RUN])
    dft, q_here, g_here, gain_here, taps, all_spec, rest_spec, own_conv = call(
        own_kernel,
        "own_conv",
        [(dft.shape, dft.dtype), act, act, row, spec, spec, spec, wide],
        8 * unit,
        (dft, filt, q_act, grad_out, gain_row),
        (seg, prod),
        [pltpu.VMEM(filt.shape, filt.dtype), pltpu.SemaphoreType.DMA((5,))],
    )
    conv, all_spec, stats = call(
        halo_kernel,
        "halo_conv",
        [wide, spec, ((n_x, 2, ROWS), jnp.float32)],
        3 * unit,
        (),
        (dft, seg, halo, far_halo, taps, all_spec, own_conv, q_here, g_here, gain_here),
    )
    here = lax.all_to_all(stats, "x", 0, 0, tiled=True)
    there = lax.ppermute(here, "z_hi", [(0, 1), (1, 0)])

    groups = (8, width // ROWS, 9, 2, ROWS)
    chunks, head = call(
        filter_kernel,
        "filter_grad",
        [(groups, jnp.bfloat16), act],
        5 * unit,
        (),
        (dft, seg, here, there, conv, all_spec, rest_spec, q_here, g_here, gain_here),
    )
    parts = lax.all_to_all(chunks.reshape(n_ctx, 9, 2, ROWS), "ctx", 0, 0, tiled=True)
    parts, head = lax.optimization_barrier((parts, head))
    some = [pltpu.VMEM((n_ctx // COPIES, 9, 2, ROWS), jnp.bfloat16), pltpu.SemaphoreType.DMA((COPIES,))]
    (total,) = call(total_kernel, "total", [(parts.shape, parts.dtype)], 2**18, (), (parts,), some, False, 1)
    full = lax.all_to_all(total, "ctx", 0, 0, tiled=True)
    tail = lax.ppermute(head, "ctx", [(target, source) for source, target in edges])
    layer_out, q_grad, own_dprod, k_here, v_here = call(
        out_kernel,
        "out_grads",
        [act, act, wide, act, act],
        6 * unit,
        (q_act, grad_out, k_act, v_act),
        (dft, seg, here, there, conv, taps, gain_here),
        [mine, mine, pltpu.SemaphoreType.DMA((4,))],
        False,
    )
    k_grad, v_grad = call(
        input_kernel, "input_grads", [act, act], 3 * unit, (), (dft, seg, own_dprod, tail, taps, k_here, v_here), (), False
    )
    filt_grad, gain_grad = call(
        gather_kernel, "gather", [wide, row], 2**18, (), (full.reshape(groups),), (), False
    )
    return (layer_out, q_grad, k_grad, v_grad, filt_grad, gain_grad.reshape(width))


def solution(mesh):
    n_ctx, n_hid = mesh.shape["ctx"], mesh.shape["hid"]
    split = Mesh(mesh.devices.reshape(n_ctx, n_hid // 2, 2), ("ctx", *HID))
    tile, by_hid = P("ctx", HID), P(None, HID)
    in_specs = (tile, tile, tile, by_hid, P(HID), P("ctx"), tile)
    out_specs = (tile, tile, tile, tile, by_hid, P(HID))
    return jax.shard_map(local, mesh=split, in_specs=in_specs, out_specs=out_specs, check_vma=False)
```

```python
import jax
import jax.numpy as jnp
import ml_dtypes
import numpy as np
from jax import lax
from jax.experimental import pallas as pl
from jax.experimental.pallas import tpu as pltpu
from jax.sharding import Mesh
from jax.sharding import PartitionSpec as P

C = 8192
ROWS = 128
FREQ = 128
BLOCK = 1024
PART = 512
COPIES = 4
RUN = 8
HID = ("x", "z_hi")


def split_const(matrix):
    high = matrix.astype(ml_dtypes.bfloat16)
    low = (matrix - high.astype(np.float64)).astype(ml_dtypes.bfloat16)
    return high, low


def transforms():
    omega = 2.0 * np.pi * (np.arange(FREQ) + 0.5) / (2 * FREQ)

    def at(positions):
        angle = omega[:, None] * positions[None, :]
        return np.concatenate([np.cos(angle), -np.sin(angle)], axis=0)

    here = np.arange(ROWS)
    own = at(here)
    left = at(here - ROWS)
    left[:, 0] = 0.0
    right = at(here + ROWS)
    right[:, -1] = 0.0
    own_hl = np.concatenate(split_const(own), axis=1)
    left_hl = np.concatenate(split_const(left), axis=1)
    right_hl = np.concatenate(split_const(right), axis=1)
    back_hl = np.concatenate(split_const(own.T / FREQ), axis=0)
    return np.stack([own_hl, back_hl, left_hl, right_hl])


def mm(a, b):
    return jnp.dot(a, b, preferred_element_type=jnp.float32)


def forward(matrix_hl, x):
    return mm(matrix_hl, jnp.concatenate([x, x], axis=0))


def forward_wide(matrix_hl, x):
    high = x.astype(jnp.bfloat16)
    low = (x - high.astype(jnp.float32)).astype(jnp.bfloat16)
    return forward(matrix_hl, high) + mm(matrix_hl[:, :ROWS], low)


def backward(back_hl, spectrum):
    high = spectrum.astype(jnp.bfloat16)
    low = (spectrum - high.astype(jnp.float32)).astype(jnp.bfloat16)
    both = mm(back_hl, high)
    return both[:ROWS] + both[ROWS:] + mm(back_hl[:ROWS], low)


def times(a, b):
    ar, ai, br, bi = a[:FREQ], a[FREQ:], b[:FREQ], b[FREQ:]
    return jnp.concatenate([ar * br - ai * bi, ar * bi + ai * br], axis=0)


def times_conj(a, b):
    ar, ai, br, bi = a[:FREQ], a[FREQ:], b[:FREQ], b[FREQ:]
    return jnp.concatenate([ar * br + ai * bi, ai * br - ar * bi], axis=0)


def down(row, width):
    square = jnp.broadcast_to(row, (ROWS, ROWS)).T
    return jnp.concatenate([square] * (width // ROWS), axis=1)


def first_doc(seg):
    return (seg == seg[:, :1]).astype(jnp.float32)


def last_doc(seg):
    return (seg == seg[:, ROWS - 1 :]).astype(jnp.float32)


def parity(seg):
    return (seg % 2).astype(jnp.float32)


def blocks(width, size=BLOCK):
    return [slice(i, i + size) for i in range(0, width, size)]


def lane_sum(x):
    return sum(x[:, i : i + ROWS] for i in range(0, x.shape[1], ROWS))


def fetch(pairs, sems):
    copies = [pltpu.make_async_copy(source, target, sems.at[i]) for i, (source, target) in enumerate(pairs)]
    for copy in copies:
        copy.start()
    return copies


def compose(seg_hbm, k_hbm, v_hbm, seg_ref, prod_ref, message_ref, k_ref, v_ref, sems):
    parts = blocks(k_ref.shape[1], PART)
    pairs = [(seg_hbm, seg_ref)]
    for at in parts:
        pairs += [(k_hbm.at[:, at], k_ref.at[:, at]), (v_hbm.at[:, at], v_ref.at[:, at])]
    copies = fetch(pairs, sems)
    copies[0].wait()
    seg = seg_ref[...]
    in_last = down(last_doc(seg), PART)
    is_top = lax.broadcasted_iota(jnp.int32, (ROWS, PART), 0) == 0
    mark = parity(seg[:, ROWS - 1 :])
    for i, at in enumerate(parts):
        copies[2 * i + 1].wait()
        copies[2 * i + 2].wait()
        prod = (k_ref[:, at].astype(jnp.float32) * v_ref[:, at].astype(jnp.float32)).astype(jnp.bfloat16)
        if prod_ref is not None:
            prod_ref[:, at] = prod
        message_ref[:, at] = jnp.where(is_top, mark, prod.astype(jnp.float32) * in_last).astype(jnp.bfloat16)


def far_kernel(seg_hbm, k_hbm, v_hbm, message_ref, seg_ref, k_ref, v_ref, sems):
    @pl.when(lax.axis_index("ctx") % RUN == RUN - 1)
    def _():
        compose(seg_hbm, k_hbm, v_hbm, seg_ref, None, message_ref, k_ref, v_ref, sems)


def message_kernel(seg_hbm, k_hbm, v_hbm, seg_ref, prod_ref, message_ref, k_ref, v_ref, sems):
    compose(seg_hbm, k_hbm, v_hbm, seg_ref, prod_ref, message_ref, k_ref, v_ref, sems)


def own_kernel(dft_hbm, filt_hbm, q_hbm, g_hbm, gain_hbm, seg_ref, prod_ref, dft_ref, q_ref, g_ref, gain_ref, taps_ref, all_ref, rest_ref, conv_ref, filt_ref, sems):
    copies = fetch([(dft_hbm, dft_ref), (filt_hbm, filt_ref), (q_hbm, q_ref), (g_hbm, g_ref), (gain_hbm, gain_ref)], sems)
    in_first = down(first_doc(seg_ref[...]), BLOCK)
    outside = (1.0 - in_first).astype(jnp.bfloat16)
    copies[0].wait()
    copies[1].wait()
    own, back = dft_ref[0], dft_ref[1]
    for at in blocks(prod_ref.shape[1]):
        prod = prod_ref[:, at]
        taps = forward_wide(own, filt_ref[:, at])
        all_spec = forward(own, prod)
        rest_spec = forward(own, prod * outside)
        taps_ref[:, at] = taps
        all_ref[:, at] = all_spec
        rest_ref[:, at] = rest_spec
        conv_first = backward(back, times(all_spec, taps))
        conv_rest = backward(back, times(rest_spec, taps))
        conv_ref[:, at] = jnp.where(in_first > 0.5, conv_first, conv_rest)
    for copy in copies[2:]:
        copy.wait()


def halo_kernel(dft_ref, seg_ref, near_ref, far_ref, taps_ref, own_conv_ref, q_ref, g_ref, gain_ref, conv_ref, stats_ref):
    seg = seg_ref[...]
    in_first = down(first_doc(seg), BLOCK)
    mark = parity(seg[:, :1])
    back, left = dft_ref[1], dft_ref[2]
    square, inner = 0.0, 0.0
    for at in blocks(q_ref.shape[1]):
        halo = near_ref[:, at] + far_ref[:, at]
        joined = (halo[0:1].astype(jnp.float32) == mark).astype(jnp.float32)
        halo_spec = forward(left, halo) * joined
        conv = own_conv_ref[:, at] + in_first * backward(back, times(halo_spec, taps_ref[:, at]))
        conv_ref[:, at] = conv
        y = q_ref[:, at].astype(jnp.float32) * conv
        square += lane_sum(y * y)
        inner += lane_sum(g_ref[:, at].astype(jnp.float32) * gain_ref[:, at] * y)
    rows = jnp.concatenate([jnp.sum(square.T, axis=0, keepdims=True), jnp.sum(inner.T, axis=0, keepdims=True)], axis=0)
    stats_ref[...] = jnp.broadcast_to(rows[None], stats_ref.shape)


def spectrum_kernel(dft_ref, seg_ref, near_ref, far_ref, all_ref, spec_ref):
    mark = parity(seg_ref[:, :1])
    left = dft_ref[2]
    for at in blocks(all_ref.shape[1]):
        halo = near_ref[:, at] + far_ref[:, at]
        joined = (halo[0:1].astype(jnp.float32) == mark).astype(jnp.float32)
        spec_ref[:, at] = all_ref[:, at] + forward(left, halo) * joined


def scales(stats_ref):
    total = jnp.sum(stats_ref[...], axis=0)
    rinv = lax.rsqrt(total[0:1] / C + 1e-06)
    return down(rinv, BLOCK), down(rinv * rinv * rinv * total[1:2] / C, BLOCK)


def filter_kernel(dft_ref, seg_ref, stats_ref, conv_ref, spec_ref, rest_ref, q_ref, g_ref, gain_ref, chunk_ref, head_ref):
    rinv, slope = scales(stats_ref)
    seg = seg_ref[...]
    first = down(first_doc(seg), BLOCK).astype(jnp.bfloat16)
    is_end = lax.broadcasted_iota(jnp.int32, (ROWS, BLOCK), 0) == ROWS - 1
    mark = parity(seg[:, :1])
    own, back = dft_ref[0], dft_ref[1]
    for step, at in enumerate(blocks(q_ref.shape[1])):
        query = q_ref[:, at].astype(jnp.float32)
        up = g_ref[:, at].astype(jnp.float32)
        y = query * conv_ref[:, at]
        dy = rinv * (up * gain_ref[:, at]) - y * slope
        dconv = (dy * query).astype(jnp.bfloat16)
        d_first = dconv * first
        head_ref[:, at] = jnp.where(is_end, mark, d_first.astype(jnp.float32)).astype(jnp.bfloat16)
        first_spec = forward(own, d_first)
        rest_spec = forward(own, dconv - d_first)
        spectrum = times_conj(first_spec, spec_ref[:, at]) + times_conj(rest_spec, rest_ref[:, at])
        taps = backward(back, spectrum).astype(jnp.bfloat16)
        gain_sum = jnp.sum(up * y * rinv, axis=0, keepdims=True)
        gain_high = gain_sum.astype(jnp.bfloat16)
        gain_low = (gain_sum - gain_high.astype(jnp.float32)).astype(jnp.bfloat16)
        gain_both = jnp.concatenate([gain_high, gain_low], axis=0)
        for sub in range(BLOCK // ROWS):
            lanes = slice(sub * ROWS, (sub + 1) * ROWS)
            block = step * (BLOCK // ROWS) + sub
            for group in range(8):
                for pair in range(8):
                    row = group * 16 + pair * 2
                    chunk_ref[group, block, pair] = taps[row : row + 2, lanes]
                chunk_ref[group, block, 8] = gain_both[:, lanes]


def out_kernel(q_hbm, g_hbm, k_hbm, v_hbm, dft_ref, seg_ref, stats_ref, conv_ref, taps_ref, gain_ref, layer_ref, qg_ref, dprod_ref, k_ref, v_ref, q_ref, g_ref, sems):
    copies = fetch([(q_hbm, q_ref), (g_hbm, g_ref), (k_hbm, k_ref), (v_hbm, v_ref)], sems)
    rinv, slope = scales(stats_ref)
    seg = seg_ref[...]
    in_last = down(last_doc(seg), BLOCK)
    in_first = down(first_doc(seg), BLOCK).astype(jnp.bfloat16)
    own, back = dft_ref[0], dft_ref[1]
    copies[0].wait()
    copies[1].wait()
    for at in blocks(q_ref.shape[1]):
        query, conv, gain = q_ref[:, at].astype(jnp.float32), conv_ref[:, at], gain_ref[:, at]
        y = query * conv
        dy = rinv * (g_ref[:, at].astype(jnp.float32) * gain) - y * slope
        layer_ref[:, at] = (y * rinv * gain).astype(jnp.bfloat16)
        qg_ref[:, at] = (dy * conv).astype(jnp.bfloat16)
        dconv = (dy * query).astype(jnp.bfloat16)
        taps = taps_ref[:, at]
        dprod_last = backward(back, times_conj(forward(own, dconv), taps))
        dprod_first = backward(back, times_conj(forward(own, dconv * in_first), taps))
        dprod_ref[:, at] = jnp.where(in_last > 0.5, dprod_last, dprod_first)
    copies[2].wait()
    copies[3].wait()


def input_kernel(dft_ref, seg_ref, dprod_ref, tail_ref, taps_ref, k_ref, v_ref, kg_ref, vg_ref):
    seg = seg_ref[...]
    in_last = down(last_doc(seg), BLOCK)
    mark = parity(seg[:, ROWS - 1 :])
    back, right = dft_ref[1], dft_ref[3]
    for at in blocks(k_ref.shape[1]):
        tail = tail_ref[:, at]
        joined = (tail[ROWS - 1 :].astype(jnp.float32) == mark).astype(jnp.float32)
        tail_spec = forward(right, tail) * joined
        dprod = dprod_ref[:, at] + in_last * backward(back, times_conj(tail_spec, taps_ref[:, at]))
        kg_ref[:, at] = (dprod * v_ref[:, at].astype(jnp.float32)).astype(jnp.bfloat16)
        vg_ref[:, at] = (dprod * k_ref[:, at].astype(jnp.float32)).astype(jnp.bfloat16)


def total_kernel(parts_ref, mine_hbm, mine_ref, sems):
    total = jnp.sum(parts_ref[...].astype(jnp.float32), axis=0)
    gain = total[8, 0:1] + total[8, 1:2]
    gain_high = gain.astype(jnp.bfloat16)
    gain_low = (gain - gain_high.astype(jnp.float32)).astype(jnp.bfloat16)
    mine = jnp.concatenate([total[:8].astype(jnp.bfloat16), jnp.concatenate([gain_high, gain_low], axis=0)[None]], axis=0)
    mine_ref[...] = jnp.broadcast_to(mine[None], mine_ref.shape)
    some = mine_ref.shape[0]
    copies = fetch([(mine_ref, mine_hbm.at[pl.ds(i, some)]) for i in range(0, parts_ref.shape[0], some)], sems)
    for copy in copies:
        copy.wait()


def gather_kernel(full_ref, filt_ref, gain_ref):
    for block in range(full_ref.shape[1]):
        lanes = slice(block * ROWS, (block + 1) * ROWS)
        for group in range(8):
            for pair in range(8):
                row = group * 16 + pair * 2
                filt_ref[row : row + 2, lanes] = full_ref[group, block, pair].astype(jnp.float32)
        gain = full_ref[0, block, 8].astype(jnp.float32)
        gain_ref[:, lanes] = gain[0:1] + gain[1:2]


def call(kernel, name, outs, flops, hbm, vmem, scratch=(), pinned=True, sent=0):
    hbm = [pltpu.with_memory_space_constraint(a, pltpu.HBM) for a in hbm]
    args = (*hbm, *vmem)
    moved = sum(a.size * a.dtype.itemsize for a in args)
    here = pl.BlockSpec(memory_space=pltpu.VMEM)
    space = pltpu.VMEM if pinned else jax.ShapeDtypeStruct
    return pl.pallas_call(
        kernel,
        in_specs=[pl.BlockSpec(memory_space=pltpu.HBM)] * len(hbm) + [here] * len(vmem),
        out_specs=[pl.BlockSpec(memory_space=pltpu.HBM)] * sent + [here] * (len(outs) - sent),
        out_shape=[space(shape, dtype) for shape, dtype in outs],
        scratch_shapes=scratch,
        compiler_params=pltpu.CompilerParams(vmem_limit_bytes=32 * 1024 * 1024),
        cost_estimate=pl.CostEstimate(flops=flops, bytes_accessed=moved, transcendentals=0),
        name=name,
    )(*args)


def local(q_act, k_act, v_act, filt, gain, segments, grad_out):
    width = q_act.shape[1]
    n_ctx, n_x = lax.axis_size("ctx"), lax.axis_size("x")
    dft = jnp.asarray(transforms())
    seg = segments.reshape(1, ROWS)
    gain_row = gain.reshape(1, width)
    act = ((ROWS, width), jnp.bfloat16)
    wide = ((ROWS, width), jnp.float32)
    spec = ((2 * FREQ, width), jnp.float32)
    unit = 2**27

    row = ((1, width), jnp.float32)
    sems = pltpu.SemaphoreType.DMA((1 + 2 * (width // PART),))
    mine = pltpu.VMEM((ROWS, width), jnp.bfloat16)
    (far,) = call(
        far_kernel, "far_message", [act], 2**18, (seg, k_act, v_act), (), [pltpu.VMEM((1, ROWS), jnp.int32), mine, mine, sems]
    )
    seg, prod, message = call(
        message_kernel, "message", [((1, ROWS), jnp.int32), act, act], 2**18, (seg, k_act, v_act), (), [mine, mine, sems]
    )
    edges = [(source, source + 1) for source in range(n_ctx - 1)]
    far_halo = lax.ppermute(far, "ctx", [edge for edge in edges if edge[1] % RUN == 0])
    halo = lax.ppermute(message, "ctx", [edge for edge in edges if edge[1] % RUN])
    dft, q_here, g_here, gain_here, taps, all_spec, rest_spec, own_conv = call(
        own_kernel,
        "own_conv",
        [(dft.shape, dft.dtype), act, act, row, spec, spec, spec, wide],
        8 * unit,
        (dft, filt, q_act, grad_out, gain_row),
        (seg, prod),
        [pltpu.VMEM(filt.shape, filt.dtype), pltpu.SemaphoreType.DMA((5,))],
    )
    conv, stats = call(
        halo_kernel,
        "halo_conv",
        [wide, ((n_x, 2, ROWS), jnp.float32)],
        3 * unit,
        (),
        (dft, seg, halo, far_halo, taps, own_conv, q_here, g_here, gain_here),
    )
    all_spec = call(spectrum_kernel, "spectrum", [spec], unit, (), (dft, seg, halo, far_halo, all_spec))[0]
    stats = stats + lax.ppermute(stats, "z_hi", [(0, 1), (1, 0)])
    stats, all_spec = lax.optimization_barrier((stats, all_spec))
    stats = lax.all_to_all(stats, "x", 0, 0, tiled=True)

    groups = (8, width // ROWS, 9, 2, ROWS)
    chunks, head = call(
        filter_kernel,
        "filter_grad",
        [(groups, jnp.bfloat16), act],
        5 * unit,
        (),
        (dft, seg, stats, conv, all_spec, rest_spec, q_here, g_here, gain_here),
    )
    parts = lax.all_to_all(chunks.reshape(n_ctx, 9, 2, ROWS), "ctx", 0, 0, tiled=True)
    parts, head = lax.optimization_barrier((parts, head))
    some = [pltpu.VMEM((n_ctx // COPIES, 9, 2, ROWS), jnp.bfloat16), pltpu.SemaphoreType.DMA((COPIES,))]
    (total,) = call(total_kernel, "total", [(parts.shape, parts.dtype)], 2**18, (), (parts,), some, False, 1)
    full = lax.all_to_all(total, "ctx", 0, 0, tiled=True)
    tail = lax.ppermute(head, "ctx", [(target, source) for source, target in edges])
    layer_out, q_grad, own_dprod, k_here, v_here = call(
        out_kernel,
        "out_grads",
        [act, act, wide, act, act],
        6 * unit,
        (q_act, grad_out, k_act, v_act),
        (dft, seg, stats, conv, taps, gain_here),
        [mine, mine, pltpu.SemaphoreType.DMA((4,))],
        False,
    )
    k_grad, v_grad = call(
        input_kernel, "input_grads", [act, act], 3 * unit, (), (dft, seg, own_dprod, tail, taps, k_here, v_here), (), False
    )
    filt_grad, gain_grad = call(
        gather_kernel, "gather", [wide, row], 2**18, (), (full.reshape(groups),), (), False
    )
    return (layer_out, q_grad, k_grad, v_grad, filt_grad, gain_grad.reshape(width))


def solution(mesh):
    n_ctx, n_hid = mesh.shape["ctx"], mesh.shape["hid"]
    split = Mesh(mesh.devices.reshape(n_ctx, n_hid // 2, 2), ("ctx", *HID))
    tile, by_hid = P("ctx", HID), P(None, HID)
    in_specs = (tile, tile, tile, by_hid, P(HID), P("ctx"), tile)
    out_specs = (tile, tile, tile, tile, by_hid, P(HID))
    return jax.shard_map(local, mesh=split, in_specs=in_specs, out_specs=out_specs, check_vma=False)
```

```python
import jax
import jax.numpy as jnp
import ml_dtypes
import numpy as np
from jax import lax
from jax.experimental import pallas as pl
from jax.experimental.pallas import tpu as pltpu
from jax.sharding import Mesh
from jax.sharding import PartitionSpec as P

C = 8192
ROWS = 128
FREQ = 128
BLOCK = 1024
PART = 512
COPIES = 4
RUN = 8
HID = ("x", "z_hi")


def split_const(matrix):
    high = matrix.astype(ml_dtypes.bfloat16)
    low = (matrix - high.astype(np.float64)).astype(ml_dtypes.bfloat16)
    return high, low


def transforms():
    omega = 2.0 * np.pi * (np.arange(FREQ) + 0.5) / (2 * FREQ)

    def at(positions):
        angle = omega[:, None] * positions[None, :]
        return np.concatenate([np.cos(angle), -np.sin(angle)], axis=0)

    here = np.arange(ROWS)
    own = at(here)
    left = at(here - ROWS)
    left[:, 0] = 0.0
    right = at(here + ROWS)
    right[:, -1] = 0.0
    own_hl = np.concatenate(split_const(own), axis=1)
    left_hl = np.concatenate(split_const(left), axis=1)
    right_hl = np.concatenate(split_const(right), axis=1)
    back_hl = np.concatenate(split_const(own.T / FREQ), axis=0)
    return np.stack([own_hl, back_hl, left_hl, right_hl])


def mm(a, b):
    return jnp.dot(a, b, preferred_element_type=jnp.float32)


def forward(matrix_hl, x):
    return mm(matrix_hl, jnp.concatenate([x, x], axis=0))


def forward_wide(matrix_hl, x):
    high = x.astype(jnp.bfloat16)
    low = (x - high.astype(jnp.float32)).astype(jnp.bfloat16)
    return forward(matrix_hl, high) + mm(matrix_hl[:, :ROWS], low)


def backward(back_hl, spectrum):
    high = spectrum.astype(jnp.bfloat16)
    low = (spectrum - high.astype(jnp.float32)).astype(jnp.bfloat16)
    both = mm(back_hl, high)
    return both[:ROWS] + both[ROWS:] + mm(back_hl[:ROWS], low)


def times(a, b):
    ar, ai, br, bi = a[:FREQ], a[FREQ:], b[:FREQ], b[FREQ:]
    return jnp.concatenate([ar * br - ai * bi, ar * bi + ai * br], axis=0)


def times_conj(a, b):
    ar, ai, br, bi = a[:FREQ], a[FREQ:], b[:FREQ], b[FREQ:]
    return jnp.concatenate([ar * br + ai * bi, ai * br - ar * bi], axis=0)


def down(row, width):
    square = jnp.broadcast_to(row, (ROWS, ROWS)).T
    return jnp.concatenate([square] * (width // ROWS), axis=1)


def first_doc(seg):
    return (seg == seg[:, :1]).astype(jnp.float32)


def last_doc(seg):
    return (seg == seg[:, ROWS - 1 :]).astype(jnp.float32)


def parity(seg):
    return (seg % 2).astype(jnp.float32)


def blocks(width, size=BLOCK):
    return [slice(i, i + size) for i in range(0, width, size)]


def lane_sum(x):
    return sum(x[:, i : i + ROWS] for i in range(0, x.shape[1], ROWS))


def fetch(pairs, sems):
    copies = [pltpu.make_async_copy(source, target, sems.at[i]) for i, (source, target) in enumerate(pairs)]
    for copy in copies:
        copy.start()
    return copies


def compose(seg_hbm, k_hbm, v_hbm, seg_ref, prod_ref, message_ref, k_ref, v_ref, sems):
    parts = blocks(k_ref.shape[1], PART)
    pairs = [(seg_hbm, seg_ref)]
    for at in parts:
        pairs += [(k_hbm.at[:, at], k_ref.at[:, at]), (v_hbm.at[:, at], v_ref.at[:, at])]
    copies = fetch(pairs, sems)
    copies[0].wait()
    seg = seg_ref[...]
    in_last = down(last_doc(seg), PART)
    is_top = lax.broadcasted_iota(jnp.int32, (ROWS, PART), 0) == 0
    mark = parity(seg[:, ROWS - 1 :])
    for i, at in enumerate(parts):
        copies[2 * i + 1].wait()
        copies[2 * i + 2].wait()
        prod = (k_ref[:, at].astype(jnp.float32) * v_ref[:, at].astype(jnp.float32)).astype(jnp.bfloat16)
        if prod_ref is not None:
            prod_ref[:, at] = prod
        message_ref[:, at] = jnp.where(is_top, mark, prod.astype(jnp.float32) * in_last).astype(jnp.bfloat16)


def far_kernel(seg_hbm, k_hbm, v_hbm, message_ref, seg_ref, k_ref, v_ref, sems):
    @pl.when(lax.axis_index("ctx") % RUN == RUN - 1)
    def _():
        compose(seg_hbm, k_hbm, v_hbm, seg_ref, None, message_ref, k_ref, v_ref, sems)


def message_kernel(seg_hbm, k_hbm, v_hbm, seg_ref, prod_ref, message_ref, k_ref, v_ref, sems):
    compose(seg_hbm, k_hbm, v_hbm, seg_ref, prod_ref, message_ref, k_ref, v_ref, sems)


def own_kernel(dft_hbm, filt_hbm, q_hbm, g_hbm, gain_hbm, seg_ref, prod_ref, dft_ref, q_ref, g_ref, gain_ref, taps_ref, all_ref, rest_ref, conv_ref, filt_ref, sems):
    copies = fetch([(dft_hbm, dft_ref), (filt_hbm, filt_ref), (q_hbm, q_ref), (g_hbm, g_ref), (gain_hbm, gain_ref)], sems)
    in_first = down(first_doc(seg_ref[...]), BLOCK)
    outside = (1.0 - in_first).astype(jnp.bfloat16)
    copies[0].wait()
    copies[1].wait()
    own, back = dft_ref[0], dft_ref[1]
    for at in blocks(prod_ref.shape[1]):
        prod = prod_ref[:, at]
        taps = forward_wide(own, filt_ref[:, at])
        all_spec = forward(own, prod)
        rest_spec = forward(own, prod * outside)
        taps_ref[:, at] = taps
        all_ref[:, at] = all_spec
        rest_ref[:, at] = rest_spec
        conv_first = backward(back, times(all_spec, taps))
        conv_rest = backward(back, times(rest_spec, taps))
        conv_ref[:, at] = jnp.where(in_first > 0.5, conv_first, conv_rest)
    for copy in copies[2:]:
        copy.wait()


def halo_kernel(dft_ref, seg_ref, near_ref, far_ref, taps_ref, all_ref, own_conv_ref, q_ref, g_ref, gain_ref, conv_ref, spec_ref, stats_ref):
    seg = seg_ref[...]
    in_first = down(first_doc(seg), BLOCK)
    mark = parity(seg[:, :1])
    back, left = dft_ref[1], dft_ref[2]
    square, inner = 0.0, 0.0
    for at in blocks(q_ref.shape[1]):
        halo = near_ref[:, at] + far_ref[:, at]
        joined = (halo[0:1].astype(jnp.float32) == mark).astype(jnp.float32)
        halo_spec = forward(left, halo) * joined
        spec_ref[:, at] = all_ref[:, at] + halo_spec
        conv = own_conv_ref[:, at] + in_first * backward(back, times(halo_spec, taps_ref[:, at]))
        conv_ref[:, at] = conv
        y = q_ref[:, at].astype(jnp.float32) * conv
        square += lane_sum(y * y)
        inner += lane_sum(g_ref[:, at].astype(jnp.float32) * gain_ref[:, at] * y)
    rows = jnp.concatenate([jnp.sum(square.T, axis=0, keepdims=True), jnp.sum(inner.T, axis=0, keepdims=True)], axis=0)
    stats_ref[...] = jnp.broadcast_to(rows[None], stats_ref.shape)


def scales(stats_ref):
    total = jnp.sum(stats_ref[...], axis=0)
    rinv = lax.rsqrt(total[0:1] / C + 1e-06)
    return down(rinv, BLOCK), down(rinv * rinv * rinv * total[1:2] / C, BLOCK)


def filter_kernel(dft_ref, seg_ref, stats_ref, conv_ref, spec_ref, rest_ref, q_ref, g_ref, gain_ref, chunk_ref, head_ref):
    rinv, slope = scales(stats_ref)
    seg = seg_ref[...]
    first = down(first_doc(seg), BLOCK).astype(jnp.bfloat16)
    is_end = lax.broadcasted_iota(jnp.int32, (ROWS, BLOCK), 0) == ROWS - 1
    mark = parity(seg[:, :1])
    own, back = dft_ref[0], dft_ref[1]
    for step, at in enumerate(blocks(q_ref.shape[1])):
        query = q_ref[:, at].astype(jnp.float32)
        up = g_ref[:, at].astype(jnp.float32)
        y = query * conv_ref[:, at]
        dy = rinv * (up * gain_ref[:, at]) - y * slope
        dconv = (dy * query).astype(jnp.bfloat16)
        d_first = dconv * first
        head_ref[:, at] = jnp.where(is_end, mark, d_first.astype(jnp.float32)).astype(jnp.bfloat16)
        first_spec = forward(own, d_first)
        rest_spec = forward(own, dconv - d_first)
        spectrum = times_conj(first_spec, spec_ref[:, at]) + times_conj(rest_spec, rest_ref[:, at])
        taps = backward(back, spectrum).astype(jnp.bfloat16)
        gain_sum = jnp.sum(up * y * rinv, axis=0, keepdims=True)
        gain_high = gain_sum.astype(jnp.bfloat16)
        gain_low = (gain_sum - gain_high.astype(jnp.float32)).astype(jnp.bfloat16)
        gain_both = jnp.concatenate([gain_high, gain_low], axis=0)
        for sub in range(BLOCK // ROWS):
            lanes = slice(sub * ROWS, (sub + 1) * ROWS)
            block = step * (BLOCK // ROWS) + sub
            for group in range(8):
                for pair in range(8):
                    row = group * 16 + pair * 2
                    chunk_ref[group, block, pair] = taps[row : row + 2, lanes]
                chunk_ref[group, block, 8] = gain_both[:, lanes]


def out_kernel(q_hbm, g_hbm, k_hbm, v_hbm, dft_ref, seg_ref, stats_ref, conv_ref, taps_ref, gain_ref, layer_ref, qg_ref, dprod_ref, k_ref, v_ref, q_ref, g_ref, sems):
    copies = fetch([(q_hbm, q_ref), (g_hbm, g_ref), (k_hbm, k_ref), (v_hbm, v_ref)], sems)
    rinv, slope = scales(stats_ref)
    seg = seg_ref[...]
    in_last = down(last_doc(seg), BLOCK)
    in_first = down(first_doc(seg), BLOCK).astype(jnp.bfloat16)
    own, back = dft_ref[0], dft_ref[1]
    copies[0].wait()
    copies[1].wait()
    for at in blocks(q_ref.shape[1]):
        query, conv, gain = q_ref[:, at].astype(jnp.float32), conv_ref[:, at], gain_ref[:, at]
        y = query * conv
        dy = rinv * (g_ref[:, at].astype(jnp.float32) * gain) - y * slope
        layer_ref[:, at] = (y * rinv * gain).astype(jnp.bfloat16)
        qg_ref[:, at] = (dy * conv).astype(jnp.bfloat16)
        dconv = (dy * query).astype(jnp.bfloat16)
        taps = taps_ref[:, at]
        dprod_last = backward(back, times_conj(forward(own, dconv), taps))
        dprod_first = backward(back, times_conj(forward(own, dconv * in_first), taps))
        dprod_ref[:, at] = jnp.where(in_last > 0.5, dprod_last, dprod_first)
    copies[2].wait()
    copies[3].wait()


def input_kernel(dft_ref, seg_ref, dprod_ref, tail_ref, taps_ref, k_ref, v_ref, kg_ref, vg_ref):
    seg = seg_ref[...]
    in_last = down(last_doc(seg), BLOCK)
    mark = parity(seg[:, ROWS - 1 :])
    back, right = dft_ref[1], dft_ref[3]
    for at in blocks(k_ref.shape[1]):
        tail = tail_ref[:, at]
        joined = (tail[ROWS - 1 :].astype(jnp.float32) == mark).astype(jnp.float32)
        tail_spec = forward(right, tail) * joined
        dprod = dprod_ref[:, at] + in_last * backward(back, times_conj(tail_spec, taps_ref[:, at]))
        kg_ref[:, at] = (dprod * v_ref[:, at].astype(jnp.float32)).astype(jnp.bfloat16)
        vg_ref[:, at] = (dprod * k_ref[:, at].astype(jnp.float32)).astype(jnp.bfloat16)


def total_kernel(parts_ref, mine_hbm, mine_ref, sems):
    total = jnp.sum(parts_ref[...].astype(jnp.float32), axis=0)
    gain = total[8, 0:1] + total[8, 1:2]
    gain_high = gain.astype(jnp.bfloat16)
    gain_low = (gain - gain_high.astype(jnp.float32)).astype(jnp.bfloat16)
    mine = jnp.concatenate([total[:8].astype(jnp.bfloat16), jnp.concatenate([gain_high, gain_low], axis=0)[None]], axis=0)
    mine_ref[...] = jnp.broadcast_to(mine[None], mine_ref.shape)
    some = mine_ref.shape[0]
    copies = fetch([(mine_ref, mine_hbm.at[pl.ds(i, some)]) for i in range(0, parts_ref.shape[0], some)], sems)
    for copy in copies:
        copy.wait()


def gather_kernel(full_ref, filt_ref, gain_ref):
    for block in range(full_ref.shape[1]):
        lanes = slice(block * ROWS, (block + 1) * ROWS)
        for group in range(8):
            for pair in range(8):
                row = group * 16 + pair * 2
                filt_ref[row : row + 2, lanes] = full_ref[group, block, pair].astype(jnp.float32)
        gain = full_ref[0, block, 8].astype(jnp.float32)
        gain_ref[:, lanes] = gain[0:1] + gain[1:2]


def call(kernel, name, outs, flops, hbm, vmem, scratch=(), pinned=True, sent=0):
    hbm = [pltpu.with_memory_space_constraint(a, pltpu.HBM) for a in hbm]
    args = (*hbm, *vmem)
    moved = sum(a.size * a.dtype.itemsize for a in args)
    here = pl.BlockSpec(memory_space=pltpu.VMEM)
    space = pltpu.VMEM if pinned else jax.ShapeDtypeStruct
    return pl.pallas_call(
        kernel,
        in_specs=[pl.BlockSpec(memory_space=pltpu.HBM)] * len(hbm) + [here] * len(vmem),
        out_specs=[pl.BlockSpec(memory_space=pltpu.HBM)] * sent + [here] * (len(outs) - sent),
        out_shape=[space(shape, dtype) for shape, dtype in outs],
        scratch_shapes=scratch,
        compiler_params=pltpu.CompilerParams(vmem_limit_bytes=32 * 1024 * 1024),
        cost_estimate=pl.CostEstimate(flops=flops, bytes_accessed=moved, transcendentals=0),
        name=name,
    )(*args)


def local(q_act, k_act, v_act, filt, gain, segments, grad_out):
    width = q_act.shape[1]
    n_ctx, n_x = lax.axis_size("ctx"), lax.axis_size("x")
    dft = jnp.asarray(transforms())
    seg = segments.reshape(1, ROWS)
    gain_row = gain.reshape(1, width)
    act = ((ROWS, width), jnp.bfloat16)
    wide = ((ROWS, width), jnp.float32)
    spec = ((2 * FREQ, width), jnp.float32)
    unit = 2**27

    row = ((1, width), jnp.float32)
    sems = pltpu.SemaphoreType.DMA((1 + 2 * (width // PART),))
    mine = pltpu.VMEM((ROWS, width), jnp.bfloat16)
    (far,) = call(
        far_kernel, "far_message", [act], 2**18, (seg, k_act, v_act), (), [pltpu.VMEM((1, ROWS), jnp.int32), mine, mine, sems]
    )
    seg, prod, message = call(
        message_kernel, "message", [((1, ROWS), jnp.int32), act, act], 2**18, (seg, k_act, v_act), (), [mine, mine, sems]
    )
    edges = [(source, source + 1) for source in range(n_ctx - 1)]
    far_halo = lax.ppermute(far, "ctx", [edge for edge in edges if edge[1] % RUN == 0])
    halo = lax.ppermute(message, "ctx", [edge for edge in edges if edge[1] % RUN])
    dft, q_here, g_here, gain_here, taps, all_spec, rest_spec, own_conv = call(
        own_kernel,
        "own_conv",
        [(dft.shape, dft.dtype), act, act, row, spec, spec, spec, wide],
        8 * unit,
        (dft, filt, q_act, grad_out, gain_row),
        (seg, prod),
        [pltpu.VMEM(filt.shape, filt.dtype), pltpu.SemaphoreType.DMA((5,))],
    )
    conv, all_spec, stats = call(
        halo_kernel,
        "halo_conv",
        [wide, spec, ((n_x, 2, ROWS), jnp.float32)],
        3 * unit,
        (),
        (dft, seg, halo, far_halo, taps, all_spec, own_conv, q_here, g_here, gain_here),
    )
    stats = stats + lax.ppermute(stats, "z_hi", [(0, 1), (1, 0)])
    stats = lax.all_to_all(stats, "x", 0, 0, tiled=True)

    groups = (8, width // ROWS, 9, 2, ROWS)
    chunks, head = call(
        filter_kernel,
        "filter_grad",
        [(groups, jnp.bfloat16), act],
        5 * unit,
        (),
        (dft, seg, stats, conv, all_spec, rest_spec, q_here, g_here, gain_here),
    )
    parts = lax.all_to_all(chunks.reshape(n_ctx, 9, 2, ROWS), "ctx", 0, 0, tiled=True)
    parts, head = lax.optimization_barrier((parts, head))
    some = [pltpu.VMEM((n_ctx // COPIES, 9, 2, ROWS), jnp.bfloat16), pltpu.SemaphoreType.DMA((COPIES,))]
    (total,) = call(total_kernel, "total", [(parts.shape, parts.dtype)], 2**18, (), (parts,), some, False, 1)
    full = lax.all_to_all(total, "ctx", 0, 0, tiled=True)
    tail = lax.ppermute(head, "ctx", [(target, source) for source, target in edges])
    layer_out, q_grad, own_dprod, k_here, v_here = call(
        out_kernel,
        "out_grads",
        [act, act, wide, act, act],
        6 * unit,
        (q_act, grad_out, k_act, v_act),
        (dft, seg, stats, conv, taps, gain_here),
        [mine, mine, pltpu.SemaphoreType.DMA((4,))],
        False,
    )
    k_grad, v_grad = call(
        input_kernel, "input_grads", [act, act], 3 * unit, (), (dft, seg, own_dprod, tail, taps, k_here, v_here), (), False
    )
    filt_grad, gain_grad = call(
        gather_kernel, "gather", [wide, row], 2**18, (), (full.reshape(groups),), (), False
    )
    return (layer_out, q_grad, k_grad, v_grad, filt_grad, gain_grad.reshape(width))


def solution(mesh):
    n_ctx, n_hid = mesh.shape["ctx"], mesh.shape["hid"]
    split = Mesh(mesh.devices.reshape(n_ctx, n_hid // 2, 2), ("ctx", *HID))
    tile, by_hid = P("ctx", HID), P(None, HID)
    in_specs = (tile, tile, tile, by_hid, P(HID), P("ctx"), tile)
    out_specs = (tile, tile, tile, tile, by_hid, P(HID))
    return jax.shard_map(local, mesh=split, in_specs=in_specs, out_specs=out_specs, check_vma=False)
```
